32 devices in a mesh: pole: 4 (over x, core), slab: 8 (over z, y).
Axes of the slice: x: 2, y: 2, z: 4, core: 2. Of those that a mesh axis runs over, the one named last changes fastest.
Arguments:
- vectors: float32 [2, 16, 32, 16, 128], P(None, None, 'slab'), may hold values from -6 to 6
- potential: float32 [32, 16, 128], P('slab'), may hold values from 0 to 2
Outputs:
- filtered: float32 [2, 16, 32, 16, 128], P(None, None, 'slab', 'pole')
- gram_correlation: float32 [2, 16, 16], replicated
- gram_energy: float32 [2, 16, 16], replicated
The draws below stay inside these ranges and needn't reach their ends.
All inputs are finite; a program needn't handle non-finite values.
Results may differ from the reference program's by a relative error of at most 0.005.
Values sent between devices are 32-bit elements; how exact they have to be, the bound alone decides.
A program may use at most 64 MiB of HBM per device.

```python
import math
import jax
import jax.numpy as jnp
from jax import lax

NB = 16
NX = 16
NY = 128
ITERS = 3
POLES = 4
NZ = 32


def shard_levels(own_key, shape, pieces, low, largest):
    gain, own = 1.0, jax.random.fold_in(own_key, 6)
    for dim, blocks in pieces:
        draws = jnp.exp(jax.random.uniform(jax.random.fold_in(own, dim), (blocks,), jnp.float32, low / len(pieces), largest / len(pieces)))
        gain = gain * jnp.repeat(draws, shape[dim] // blocks).reshape([-1 if axis == dim else 1 for axis in range(len(shape))])
    return gain


def normal_values(stream_key, extent, width, reach, split=(), kind=jnp.bfloat16):
    gain = shard_levels(stream_key, extent, split, -0.22, 0.18) if split else 1.0
    array = jax.random.normal(stream_key, extent, jnp.float32) * width * gain
    return jnp.minimum(jnp.maximum(array, -reach), reach).astype(kind)


def setup_inputs(seed: int = 0) -> dict:
    splits = jax.random.split(jax.random.key(seed), 3)
    return {
        "vectors": normal_values(splits[0], (2, NB, NZ, NX, NY), 1.0, 6.0, ((2, 8),), jnp.float32),
        "potential": jnp.clip(2.0 * jax.random.uniform(splits[1], (NZ, NX, NY), jnp.float32) ** shard_levels(splits[1], (NZ, NX, NY), ((0, 8),), -0.2, 0.2), 0.0, 2.0),
    }


contour_center = 2.0
contour_radius = 1.5


def apply_shifted(block, potential, shift_re, shift_im):
    beside = jnp.roll(block, 1, 2) + jnp.roll(block, -1, 2)
    beside = beside + jnp.roll(block, 1, 3) + jnp.roll(block, -1, 3)
    beside = beside + jnp.roll(block, 1, 4) + jnp.roll(block, -1, 4)
    diagonal = shift_re - 3.0 - potential
    real_part = diagonal * block[0] - shift_im * block[1] + 0.5 * beside[0]
    imag_part = diagonal * block[1] + shift_im * block[0] + 0.5 * beside[1]
    return jnp.stack([real_part, imag_part])


def bilinear(left, right):
    real_part = jnp.sum(left[0] * right[0] - left[1] * right[1], axis=(1, 2, 3))
    imag_part = jnp.sum(left[0] * right[1] + left[1] * right[0], axis=(1, 2, 3))
    return jnp.stack([real_part, imag_part])


def complex_divide(numer, denom):
    magnitude = denom[0] * denom[0] + denom[1] * denom[1]
    return jnp.stack([(numer[0] * denom[0] + numer[1] * denom[1]) / magnitude,
                      (numer[1] * denom[0] - numer[0] * denom[1]) / magnitude])


def column_scale(coef, block):
    first = coef[0][:, None, None, None]
    second = coef[1][:, None, None, None]
    return jnp.stack([first * block[0] - second * block[1], first * block[1] + second * block[0]])


def scalar_scale(first, second, block):
    return jnp.stack([first * block[0] - second * block[1], first * block[1] + second * block[0]])


def inner(left, right):
    return lax.dot_general(left, right, (((1,), (1,)), ((), ())), precision=lax.Precision.HIGHEST,
                           preferred_element_type=jnp.float32)


def gram_pair(filtered, image, cells):
    count = filtered.shape[1]
    sre = filtered[0].reshape(count, -1)
    sim = filtered[1].reshape(count, -1)
    hre = image[0].reshape(count, -1)
    him = image[1].reshape(count, -1)
    correlation = jnp.stack([inner(sre, sre) + inner(sim, sim), inner(sre, sim) - inner(sim, sre)]) / cells
    energy = jnp.stack([inner(sre, hre) + inner(sim, him), inner(sre, him) - inner(sim, hre)]) / cells
    return correlation, energy


def reference(vectors, potential):
    angles = (2.0 * math.pi / POLES) * (jnp.arange(POLES, dtype=jnp.float32) + 0.5)
    cosines = jnp.cos(angles)
    sines = jnp.sin(angles)
    start = vectors
    filtered = jnp.zeros_like(start)
    image = jnp.zeros_like(start)
    for pole_id in range(POLES):
        shift_re = contour_center + contour_radius * cosines[pole_id]
        shift_im = contour_radius * sines[pole_id]
        weight_re = contour_radius * cosines[pole_id] / POLES
        weight_im = contour_radius * sines[pole_id] / POLES
        solution = jnp.zeros_like(start)
        residual = start
        direction = start
        rho = bilinear(residual, residual)
        for iteration in range(ITERS):
            mapped = apply_shifted(direction, potential, shift_re, shift_im)
            alpha = complex_divide(rho, bilinear(direction, mapped))
            solution = solution + column_scale(alpha, direction)
            residual = residual - column_scale(alpha, mapped)
            if iteration + 1 < ITERS:
                rho_new = bilinear(residual, residual)
                direction = residual + column_scale(complex_divide(rho_new, rho), direction)
                rho = rho_new
        filtered = filtered + scalar_scale(weight_re, weight_im, solution)
        hsol = scalar_scale(shift_re, shift_im, solution) - start + residual
        image = image + scalar_scale(weight_re, weight_im, hsol)
    correlation, energy = gram_pair(filtered, image, NZ * NX * NY)
    return filtered, correlation, energy
```

```python
import functools
import math

import jax
import jax.numpy as jnp
from jax import lax
from jax.experimental import pallas as pl
from jax.experimental.pallas import tpu as pltpu
from jax.sharding import PartitionSpec as P

ITERS = 3
CENTER = 2.0
RADIUS = 1.5
BASE = 4.0

MESH = pl.DeviceIdType.MESH


def cmul(a, b):
    return (a[0] * b[0] - a[1] * b[1], a[0] * b[1] + a[1] * b[0])


def cmul_conj(a, b):
    return (a[0] * b[0] + a[1] * b[1], a[0] * b[1] - a[1] * b[0])


def cadd(a, b):
    return (a[0] + b[0], a[1] + b[1])


def csub(a, b):
    return (a[0] - b[0], a[1] - b[1])


def cdiv(n, d):
    inv = 1.0 / (d[0] * d[0] + d[1] * d[1])
    return ((n[0] * d[0] + n[1] * d[1]) * inv, (n[1] * d[0] - n[0] * d[1]) * inv)


def cocg_coefficients(moments, shift):
    def form(a, b):
        anti = {}
        for i, ai in enumerate(a):
            for j, bj in enumerate(b):
                term = bj if ai is None else cmul(ai, bj)
                anti[i + j] = cadd(anti[i + j], term) if i + j in anti else term
        total = None
        for n, coef in anti.items():
            term = cmul(coef, moments[n])
            total = term if total is None else cadd(total, term)
        return total

    one = (jnp.ones_like(shift[0]), jnp.zeros_like(shift[0]))
    x = []
    r = [one]
    p = [one]
    rho = moments[0]
    for iteration in range(ITERS):
        q = [cmul(shift, c) for c in p] + [None]
        for i, c in enumerate(p):
            q[i + 1] = (-c[0], -c[1]) if q[i + 1] is None else csub(q[i + 1], c)
        alpha = cdiv(rho, form(p, q))
        step = [cmul(alpha, c) for c in p]
        x = [cadd(x[i], c) if i < len(x) else c for i, c in enumerate(step)]
        if iteration + 1 < ITERS:
            down = [cmul(alpha, c) for c in q]
            r = [csub(r[i], c) if i < len(r) else (-c[0], -c[1]) for i, c in enumerate(down)]
            rho_new = form(r, r)
            beta = cdiv(rho_new, rho)
            p = [cadd(c, cmul(beta, p[i])) if i < len(p) else c for i, c in enumerate(r)]
            rho = rho_new
    return x


def kernel(
    cells, slabs, poles, v_ref, pot_ref, f_ref, corr_ref, en_ref,
    e0, e1, e2, pot_halo, diag, stack, payload, from_slab, from_pole,
    halo_send, halo_recv, slab_send, slab_recv, pole_send, pole_recv,
):
    planes, nx, lanes = pot_ref.shape
    vecs = e0.shape[2]
    nb = vecs // 2
    rows = f_ref.shape[1]
    slab = lax.axis_index("slab")
    pole = lax.axis_index("pole")
    x0 = pole * rows
    up = lax.rem(slab + 1, slabs)
    down = lax.rem(slab + slabs - 1, slabs)

    barrier = pltpu.get_barrier_semaphore()
    for d in range(1, slabs):
        pl.semaphore_signal(
            barrier, inc=1, device_id={"slab": lax.rem(slab + d, slabs)}, device_id_type=MESH
        )
    for d in range(1, poles):
        pl.semaphore_signal(
            barrier, inc=1, device_id={"pole": lax.rem(pole + d, poles)}, device_id_type=MESH
        )

    def window(q):
        return lax.rem(x0 + (q - 2 + nx), nx)

    def gather(z):
        for q in range(rows + 5):
            e0[z + 2, q] = v_ref[pl.ds(z * nx + window(q), vecs, stride=planes * nx), :]

    def halo(i, src, dst, target):
        copy = pltpu.make_async_remote_copy(
            src_ref=src, dst_ref=dst, send_sem=halo_send.at[i], recv_sem=halo_recv.at[i],
            device_id={"slab": target}, device_id_type=MESH,
        )
        copy.start()
        return copy

    def plane_rows(p, lo, hi):
        return e0.at[p, pl.ds(lo, hi - lo)]

    def send_plane(i, z, there, lo, hi, target):
        return halo(i, plane_rows(z + 2, lo, hi), plane_rows(there + 2, lo, hi), target)

    copies = []
    gather(0)
    pl.semaphore_wait(barrier, slabs - 1 + poles - 1)
    copies.append(halo(0, pot_ref.at[pl.ds(planes - 1, 1)], pot_halo.at[pl.ds(0, 1)], up))
    copies.append(halo(1, pot_ref.at[pl.ds(0, 2)], pot_halo.at[pl.ds(1, 2)], down))
    copies.append(send_plane(2, 0, planes, 0, rows + 4, down))
    gather(planes - 1)
    copies.append(send_plane(3, planes - 1, -1, 1, rows + 4, up))
    gather(1)
    copies.append(send_plane(4, 1, planes + 1, 1, rows + 3, down))
    for z in range(2, planes - 1):
        gather(z)
    copies.append(send_plane(5, planes - 2, -2, 2, rows + 3, up))
    copies.append(send_plane(6, 2, planes + 2, 2, rows + 2, down))

    def spread(ref, z, p):
        for q in range(rows + 5):
            line = ref[z, pl.ds(window(q), 1), :] - (1.0 + 0.0)
            diag[p, q] = jnp.broadcast_to(line, (vecs, lanes))

    def beside_y(block):
        flat = block.reshape(block.shape[0] * vecs, lanes)
        both = pltpu.roll(flat, 1, 1) + pltpu.roll(flat, lanes - 1, 1)
        return both.reshape(block.shape)

    def apply(src, dst, z, lo, hi):
        p = z + 2
        here = src[p, lo:hi]
        beside = src[p - 1, lo:hi] + src[p + 1, lo:hi]
        beside = beside + src[p, lo - 1:hi - 1] + src[p, lo + 1:hi + 1]
        beside = beside + beside_y(here)
        dst[p, lo:hi] = diag[p, lo:hi] * here - 0.5 * beside

    for z in range(planes):
        spread(pot_ref, z, z + 2)
    for z in range(1, planes - 1):
        apply(e0, e1, z, 1, rows + 4)
    for copy in copies:
        copy.wait_recv()
    spread(pot_halo, 0, 1)
    spread(pot_halo, 1, planes + 2)
    spread(pot_halo, 2, planes + 3)
    apply(e0, e1, -1, 2, rows + 3)
    apply(e0, e1, 0, 1, rows + 4)
    apply(e0, e1, planes - 1, 1, rows + 4)
    apply(e0, e1, planes, 1, rows + 3)
    apply(e0, e1, planes + 1, 2, rows + 2)
    for z in range(planes):
        apply(e1, e2, z, 2, rows + 3)
    apply(e1, e2, planes, 2, rows + 2)

    lo, hi = 2, rows + 2
    sums = [None] * 12
    for z in range(planes):
        p = z + 2
        u0, u1, u2 = e0[p, lo:hi], e1[p, lo:hi], e2[p, lo:hi]
        flat = u2.reshape(rows * vecs, lanes)
        ahead = pltpu.roll(flat, lanes - 1, 1).reshape(u2.shape)
        ahead = ahead + e2[p + 1, lo:hi] + e2[p, lo + 1:hi + 1]
        y = 0.5 * (diag[p, lo:hi] * u2 - ahead)
        for k, u in enumerate((u0, u1, u2, y)):
            high = u.astype(jnp.bfloat16)
            low = (u - high.astype(jnp.float32)).astype(jnp.bfloat16)
            for r in range(rows):
                at = pl.ds((z * rows + r) * lanes, lanes)
                stack[pl.ds(k * vecs, vecs), at] = high[r]
                stack[pl.ds((4 + k) * vecs, vecs), at] = low[r]
        pairs = ((u0, u0), (u0, u1), (u1, u1), (u1, u2), (u2, u2), (u2, y))
        for n, (a, b) in enumerate(pairs):
            re = a[:, :nb] * b[:, :nb] - a[:, nb:] * b[:, nb:]
            im = a[:, :nb] * b[:, nb:] + a[:, nb:] * b[:, :nb]
            re, im = jnp.sum(re, axis=0), jnp.sum(im, axis=0)
            sums[n] = re if z == 0 else sums[n] + re
            sums[6 + n] = im if z == 0 else sums[6 + n] + im

    full = lax.dot_general(
        stack[...], stack[...], (((1,), (1,)), ((), ())), preferred_element_type=jnp.float32
    )
    half = 4 * vecs
    s = full[:half, :half] + (full[:half, half:] + full[half:, :half] + full[half:, half:])

    lane = lax.broadcasted_iota(jnp.int32, (nb, lanes), 1)
    row = lax.broadcasted_iota(jnp.int32, (nb, lanes), 0)
    first = lax.rem(lane, vecs) < nb

    def hermitian(k):
        re, im = s[k * vecs:k * vecs + nb], s[k * vecs + nb:(k + 1) * vecs]
        return jnp.where(
            first, re + pltpu.roll(im, lanes - nb, 1), re - pltpu.roll(im, nb, 1)
        )

    last = hermitian(2) + jnp.where(lane >= 3 * vecs, pltpu.roll(hermitian(3), vecs, 1), 0.0)
    outer = jnp.where(lane < 2 * vecs, hermitian(0), last)
    middle = hermitian(1)
    for n in range(12):
        value = jnp.sum(sums[n], axis=1, keepdims=True)
        middle = jnp.where(lane == n, value * (2.0 if n in (5, 11) else 1.0), middle)
    payload[0, :nb] = outer
    payload[0, nb:] = middle

    def exchange(source, landing, axis, count, me, send_sem, recv_sem):
        sent = []
        for d in range(1, count):
            copy = pltpu.make_async_remote_copy(
                src_ref=source, dst_ref=landing.at[me], send_sem=send_sem.at[d],
                recv_sem=recv_sem.at[d], device_id={axis: lax.rem(me + d, count)},
                device_id_type=MESH,
            )
            copy.start()
            sent.append(copy)
        landing[me] = source[...]
        for copy in sent:
            copy.wait_recv()
        total = landing[0]
        for i in range(1, count):
            total = total + landing[i]
        return total, sent

    total, sent = exchange(payload.at[0], from_slab, "slab", slabs, slab, slab_send, slab_recv)
    copies += sent
    payload[1] = total
    total, sent = exchange(payload.at[1], from_pole, "pole", poles, pole, pole_send, pole_recv)
    copies += sent
    outer, middle = total[:nb], total[nb:]

    def column(n):
        return jnp.broadcast_to(middle[:, n:n + 1], (nb, lanes))

    moments = [(column(n), column(6 + n)) for n in range(6)]
    shift_re = jnp.zeros((nb, lanes), jnp.float32)
    shift_im, weight_re, weight_im = shift_re, shift_re, shift_re
    for j in range(poles):
        theta = 2.0 * math.pi / poles * (j + 0.5)
        c, t = math.cos(theta), math.sin(theta)
        here = lane >= 0 if j == 0 else lane == j
        shift_re = jnp.where(here, CENTER - BASE + RADIUS * c, shift_re)
        shift_im = jnp.where(here, RADIUS * t, shift_im)
        weight_re = jnp.where(lane == j, RADIUS * c / poles, weight_re)
        weight_im = jnp.where(lane == j, RADIUS * t / poles, weight_im)
    coefs = []
    for x in cocg_coefficients(moments, (shift_re, shift_im)):
        x = cmul((weight_re, weight_im), x)
        coefs.append(tuple(jnp.broadcast_to(jnp.sum(c, axis=1, keepdims=True), (nb, lanes)) for c in x))

    for z in range(planes):
        p = z + 2
        re = im = None
        for (cr, ci), e in zip(coefs, (e0, e1, e2)):
            u = e[p, lo:hi]
            ur, ui = u[:, :nb], u[:, nb:]
            tr, ti = cr * ur - ci * ui, cr * ui + ci * ur
            re, im = (tr, ti) if re is None else (re + tr, im + ti)
        f_ref[z, :, :nb] = re
        f_ref[z, :, nb:] = im

    def block(source, n):
        at = n * vecs
        return tuple(
            source if (at + o) % lanes == 0 else pltpu.roll(source, lanes - (at + o), 1)
            for o in (0, nb)
        )

    grams = [
        block(outer, 0), block(outer, 1), block(middle, 1),
        block(middle, 2), block(outer, 2), block(outer, 3),
    ]
    across = [
        tuple(jnp.sum(jnp.where(lane == row, c, 0.0), axis=0, keepdims=True) for c in coef)
        for coef in coefs
    ]

    def quadratic(first_power):
        out = None
        for l in range(3):
            term = None
            for k in range(3):
                t = cmul_conj(coefs[k], grams[k + l + first_power])
                term = t if term is None else cadd(term, t)
            term = cmul(term, across[l])
            out = term if out is None else cadd(out, term)
        return out

    corr = quadratic(0)
    energy = quadratic(1)
    for i in range(2):
        corr_ref[i] = (corr[i] / cells)[:, :nb]
        en_ref[i] = ((energy[i] + BASE * corr[i]) / cells)[:, :nb]
    for copy in copies:
        copy.wait_send()


def on_device(slabs, poles, vectors, potential):
    _, nb, planes, nx, ny = vectors.shape
    rows = nx // poles
    vecs = 2 * nb
    cells = float(planes * slabs * nx * ny)
    flat = vectors.reshape(vecs * planes * nx, ny)
    vmem = pl.BlockSpec(memory_space=pltpu.VMEM)
    field = pltpu.VMEM((planes + 5, rows + 5, vecs, ny), jnp.float32)
    dma = pltpu.SemaphoreType.DMA
    filtered, corr, energy = pl.pallas_call(
        functools.partial(kernel, cells, slabs, poles),
        out_shape=(
            jax.ShapeDtypeStruct((planes, rows, vecs, ny), jnp.float32),
            jax.ShapeDtypeStruct((2, nb, nb), jnp.float32),
            jax.ShapeDtypeStruct((2, nb, nb), jnp.float32),
        ),
        in_specs=[vmem, vmem],
        out_specs=(vmem, vmem, vmem),
        scratch_shapes=[
            field,
            field,
            field,
            pltpu.VMEM((3, nx, ny), jnp.float32),
            field,
            pltpu.VMEM((8 * vecs, planes * rows * ny), jnp.bfloat16),
            pltpu.VMEM((2, vecs, ny), jnp.float32),
            pltpu.VMEM((slabs, vecs, ny), jnp.float32),
            pltpu.VMEM((poles, vecs, ny), jnp.float32),
            dma((7,)),
            dma((7,)),
            dma((slabs,)),
            dma((slabs,)),
            dma((poles,)),
            dma((poles,)),
        ],
        compiler_params=pltpu.CompilerParams(
            collective_id=0, has_side_effects=True, vmem_limit_bytes=40 * 1024 * 1024
        ),
    )(flat, potential)
    filtered = filtered.reshape(planes, rows, 2, nb, ny).transpose(2, 3, 0, 1, 4)
    return filtered, corr, energy


def solution(mesh):
    in_specs = (P(None, None, "slab", None, None), P("slab", None, None))
    out_specs = (P(None, None, "slab", "pole", None), P(), P())
    body = functools.partial(on_device, mesh.shape["slab"], mesh.shape["pole"])
    return jax.shard_map(
        body, mesh=mesh, in_specs=in_specs, out_specs=out_specs, check_vma=False
    )
```

```python
import functools
import math

import jax
import jax.numpy as jnp
from jax import lax
from jax.experimental import pallas as pl
from jax.experimental.pallas import tpu as pltpu
from jax.sharding import PartitionSpec as P

ITERS = 3
CENTER = 2.0
RADIUS = 1.5
BASE = 4.0

MESH = pl.DeviceIdType.MESH


def cmul(a, b):
    return (a[0] * b[0] - a[1] * b[1], a[0] * b[1] + a[1] * b[0])


def cmul_conj(a, b):
    return (a[0] * b[0] + a[1] * b[1], a[0] * b[1] - a[1] * b[0])


def cadd(a, b):
    return (a[0] + b[0], a[1] + b[1])


def csub(a, b):
    return (a[0] - b[0], a[1] - b[1])


def cdiv(n, d):
    inv = 1.0 / (d[0] * d[0] + d[1] * d[1])
    return ((n[0] * d[0] + n[1] * d[1]) * inv, (n[1] * d[0] - n[0] * d[1]) * inv)


def cocg_coefficients(moments, shift):
    def form(a, b):
        anti = {}
        for i, ai in enumerate(a):
            for j, bj in enumerate(b):
                term = bj if ai is None else cmul(ai, bj)
                anti[i + j] = cadd(anti[i + j], term) if i + j in anti else term
        total = None
        for n, coef in anti.items():
            term = cmul(coef, moments[n])
            total = term if total is None else cadd(total, term)
        return total

    one = (jnp.ones_like(shift[0]), jnp.zeros_like(shift[0]))
    x = []
    r = [one]
    p = [one]
    rho = moments[0]
    for iteration in range(ITERS):
        q = [cmul(shift, c) for c in p] + [None]
        for i, c in enumerate(p):
            q[i + 1] = (-c[0], -c[1]) if q[i + 1] is None else csub(q[i + 1], c)
        alpha = cdiv(rho, form(p, q))
        step = [cmul(alpha, c) for c in p]
        x = [cadd(x[i], c) if i < len(x) else c for i, c in enumerate(step)]
        if iteration + 1 < ITERS:
            down = [cmul(alpha, c) for c in q]
            r = [csub(r[i], c) if i < len(r) else (-c[0], -c[1]) for i, c in enumerate(down)]
            rho_new = form(r, r)
            beta = cdiv(rho_new, rho)
            p = [cadd(c, cmul(beta, p[i])) if i < len(p) else c for i, c in enumerate(r)]
            rho = rho_new
    return x


def kernel(
    cells, slabs, poles, v_hbm, pot_hbm, f_ref, corr_ref, en_ref,
    v_ref, pot_ref, e0, e1, e2, pot_halo, diag, stack, payload, from_slab, from_pole,
    fetch, halo_send, halo_recv, slab_send, slab_recv, pole_send, pole_recv,
):
    planes, nx, lanes = pot_ref.shape
    vecs = e0.shape[2]
    nb = vecs // 2
    rows = f_ref.shape[1]
    slab = lax.axis_index("slab")
    pole = lax.axis_index("pole")
    x0 = pole * rows
    up = lax.rem(slab + 1, slabs)
    down = lax.rem(slab + slabs - 1, slabs)
    back = lax.rem(pole + poles - 1, poles)

    parts = fetch.shape[0] - 1
    span = vecs * planes * nx // parts
    fetches = [pltpu.make_async_copy(pot_hbm, pot_ref, fetch.at[parts])]
    for i in range(parts):
        at = pl.ds(i * span, span)
        fetches.append(pltpu.make_async_copy(v_hbm.at[at], v_ref.at[at], fetch.at[i]))
    for copy in fetches:
        copy.start()

    barrier = pltpu.get_barrier_semaphore()
    for d in range(1, slabs):
        pl.semaphore_signal(
            barrier, inc=1, device_id={"slab": lax.rem(slab + d, slabs)}, device_id_type=MESH
        )
    for d in range(1, poles):
        pl.semaphore_signal(
            barrier, inc=1, device_id={"pole": lax.rem(pole + d, poles)}, device_id_type=MESH
        )

    def window(q):
        return lax.rem(x0 + (q - 2 + nx), nx)

    def gather(z):
        for q in range(rows + 4):
            e0[z + 2, q] = v_ref[pl.ds(z * nx + window(q), vecs, stride=planes * nx), :]

    copies = []

    def send(i, src, dst, axis, target):
        copy = pltpu.make_async_remote_copy(
            src_ref=src, dst_ref=dst, send_sem=halo_send.at[i], recv_sem=halo_recv.at[i],
            device_id={axis: target}, device_id_type=MESH,
        )
        copy.start()
        copies.append(copy)
        return copy

    def send_plane(i, z, there, margin, target):
        at = pl.ds(2 - margin, rows + 2 * margin)
        return send(i, e0.at[z + 2, at], e0.at[there + 2, at], "slab", target)

    for copy in fetches:
        copy.wait()
    gather(0)
    gather(planes - 1)
    pl.semaphore_wait(barrier, slabs - 1 + poles - 1)
    near = [
        send(0, pot_ref.at[planes - 1], pot_halo.at[0], "slab", up),
        send(1, pot_ref.at[0], pot_halo.at[1], "slab", down),
        send_plane(2, planes - 1, -1, 1, up),
        send_plane(3, 0, planes, 1, down),
    ]
    for z in range(1, planes - 1):
        gather(z)
    far = [
        send_plane(4, planes - 2, -2, 0, up),
        send_plane(5, 1, planes + 1, 0, down),
    ]

    def spread(ref, z, p):
        for q in range(1, rows + 3):
            line = ref[z, pl.ds(window(q), 1), :] + (3.0 - BASE)
            diag[p, q] = jnp.broadcast_to(line, (vecs, lanes))

    def roll_y(block, by):
        flat = block.reshape(block.shape[0] * vecs, lanes)
        return pltpu.roll(flat, by, 1).reshape(block.shape)

    def apply(src, z, margin):
        p, lo, hi = z + 2, 2 - margin, rows + 2 + margin
        here = src[p, lo:hi]
        beside = src[p - 1, lo:hi] + src[p + 1, lo:hi]
        beside = beside + src[p, lo - 1:hi - 1] + src[p, lo + 1:hi + 1]
        beside = beside + (roll_y(here, 1) + roll_y(here, lanes - 1))
        return diag[p, lo:hi] * here - 0.5 * beside

    def first_power(z, margin):
        e1[z + 2, 2 - margin:rows + 2 + margin] = apply(e0, z, margin)

    def second_power(z):
        e2[z, :rows] = apply(e1, z, 0)

    for z in range(planes):
        spread(pot_ref, z, z + 2)
    for z in range(1, planes - 1):
        first_power(z, 1)
    for copy in near:
        copy.wait_recv()
    first_power(0, 1)
    first_power(planes - 1, 1)
    spread(pot_halo, 0, 1)
    spread(pot_halo, 1, planes + 2)
    for z in range(1, planes - 1):
        second_power(z)
    for copy in far:
        copy.wait_recv()
    first_power(-1, 0)
    first_power(planes, 0)
    second_power(0)
    edge = [send(6, e2.at[0, pl.ds(0, rows)], e2.at[planes, pl.ds(0, rows)], "slab", down)]
    second_power(planes - 1)
    edge.append(send(7, e2.at[pl.ds(0, planes), 0], e2.at[pl.ds(0, planes), rows], "pole", back))

    lo, hi = 2, rows + 2
    sums = [None] * 12

    def split(k, z, u):
        high = u.astype(jnp.bfloat16)
        low = (u - high.astype(jnp.float32)).astype(jnp.bfloat16)
        for r in range(rows):
            at = pl.ds((z * rows + r) * lanes, lanes)
            stack[pl.ds(k * vecs, vecs), at] = high[r]
            stack[pl.ds((4 + k) * vecs, vecs), at] = low[r]

    def collect(n, a, b):
        re = a[:, :nb] * b[:, :nb] - a[:, nb:] * b[:, nb:]
        im = a[:, :nb] * b[:, nb:] + a[:, nb:] * b[:, :nb]
        for i, value in ((n, jnp.sum(re, axis=0)), (6 + n, jnp.sum(im, axis=0))):
            sums[i] = value if sums[i] is None else sums[i] + value

    for z in range(planes):
        u0, u1, u2 = e0[z + 2, lo:hi], e1[z + 2, lo:hi], e2[z, :rows]
        for k, u in enumerate((u0, u1, u2)):
            split(k, z, u)
        for n, (a, b) in enumerate(((u0, u0), (u0, u1), (u1, u1), (u1, u2), (u2, u2))):
            collect(n, a, b)
    for copy in edge:
        copy.wait_recv()
    for z in range(planes):
        u2 = e2[z, :rows]
        ahead = e2[z + 1, :rows] + e2[z, 1:rows + 1] + roll_y(u2, lanes - 1)
        y = 0.5 * (diag[z + 2, lo:hi] * u2 - ahead)
        split(3, z, y)
        collect(5, u2, y)

    full = lax.dot_general(
        stack[...], stack[...], (((1,), (1,)), ((), ())), preferred_element_type=jnp.float32
    )
    half = 4 * vecs
    s = full[:half, :half] + (full[:half, half:] + full[half:, :half] + full[half:, half:])

    lane = lax.broadcasted_iota(jnp.int32, (nb, lanes), 1)
    row = lax.broadcasted_iota(jnp.int32, (nb, lanes), 0)
    first = lax.rem(lane, vecs) < nb

    def hermitian(k):
        re, im = s[k * vecs:k * vecs + nb], s[k * vecs + nb:(k + 1) * vecs]
        return jnp.where(
            first, re + pltpu.roll(im, lanes - nb, 1), re - pltpu.roll(im, nb, 1)
        )

    last = hermitian(2) + jnp.where(lane >= 3 * vecs, pltpu.roll(hermitian(3), vecs, 1), 0.0)
    outer = jnp.where(lane < 2 * vecs, hermitian(0), last)
    middle = hermitian(1)
    for n in range(12):
        value = jnp.sum(sums[n], axis=1, keepdims=True)
        middle = jnp.where(lane == n, value * (2.0 if n in (5, 11) else 1.0), middle)
    payload[0, :nb] = outer
    payload[0, nb:] = middle

    def exchange(source, landing, axis, count, me, send_sem, recv_sem):
        sent = []
        for d in range(1, count):
            copy = pltpu.make_async_remote_copy(
                src_ref=source, dst_ref=landing.at[me], send_sem=send_sem.at[d],
                recv_sem=recv_sem.at[d], device_id={axis: lax.rem(me + d, count)},
                device_id_type=MESH,
            )
            copy.start()
            sent.append(copy)
        landing[me] = source[...]
        for copy in sent:
            copy.wait_recv()
        total = landing[0]
        for i in range(1, count):
            total = total + landing[i]
        return total, sent

    total, sent = exchange(payload.at[0], from_slab, "slab", slabs, slab, slab_send, slab_recv)
    copies += sent
    payload[1] = total
    total, sent = exchange(payload.at[1], from_pole, "pole", poles, pole, pole_send, pole_recv)
    copies += sent
    outer, middle = total[:nb], total[nb:]

    def column(n):
        return jnp.broadcast_to(middle[:, n:n + 1], (nb, lanes))

    moments = [(column(n), column(6 + n)) for n in range(6)]
    shift_re = jnp.zeros((nb, lanes), jnp.float32)
    shift_im, weight_re, weight_im = shift_re, shift_re, shift_re
    for j in range(poles):
        theta = 2.0 * math.pi / poles * (j + 0.5)
        c, t = math.cos(theta), math.sin(theta)
        here = lane >= 0 if j == 0 else lane == j
        shift_re = jnp.where(here, CENTER - BASE + RADIUS * c, shift_re)
        shift_im = jnp.where(here, RADIUS * t, shift_im)
        weight_re = jnp.where(lane == j, RADIUS * c / poles, weight_re)
        weight_im = jnp.where(lane == j, RADIUS * t / poles, weight_im)
    coefs = []
    for x in cocg_coefficients(moments, (shift_re, shift_im)):
        x = cmul((weight_re, weight_im), x)
        coefs.append(tuple(jnp.broadcast_to(jnp.sum(c, axis=1, keepdims=True), (nb, lanes)) for c in x))

    for z in range(planes):
        p = z + 2
        re = im = None
        for (cr, ci), u in zip(coefs, (e0[p, lo:hi], e1[p, lo:hi], e2[z, :rows])):
            ur, ui = u[:, :nb], u[:, nb:]
            tr, ti = cr * ur - ci * ui, cr * ui + ci * ur
            re, im = (tr, ti) if re is None else (re + tr, im + ti)
        f_ref[z, :, :nb] = re
        f_ref[z, :, nb:] = im

    def block(source, n):
        at = n * vecs
        return tuple(
            source if (at + o) % lanes == 0 else pltpu.roll(source, lanes - (at + o), 1)
            for o in (0, nb)
        )

    grams = [
        block(outer, 0), block(outer, 1), block(middle, 1),
        block(middle, 2), block(outer, 2), block(outer, 3),
    ]
    across = [
        tuple(jnp.sum(jnp.where(lane == row, c, 0.0), axis=0, keepdims=True) for c in coef)
        for coef in coefs
    ]

    def quadratic(first_power):
        out = None
        for l in range(3):
            term = None
            for k in range(3):
                t = cmul_conj(coefs[k], grams[k + l + first_power])
                term = t if term is None else cadd(term, t)
            term = cmul(term, across[l])
            out = term if out is None else cadd(out, term)
        return out

    corr = quadratic(0)
    energy = quadratic(1)
    for i in range(2):
        corr_ref[i] = (corr[i] / cells)[:, :nb]
        en_ref[i] = ((energy[i] + BASE * corr[i]) / cells)[:, :nb]
    for copy in copies:
        copy.wait_send()


def on_device(slabs, poles, vectors, potential):
    _, nb, planes, nx, ny = vectors.shape
    rows = nx // poles
    vecs = 2 * nb
    cells = float(planes * slabs * nx * ny)
    flat = vectors.reshape(vecs * planes * nx, ny)
    vmem = pl.BlockSpec(memory_space=pltpu.VMEM)
    whole = pl.BlockSpec(memory_space=pl.ANY)
    field = pltpu.VMEM((planes + 4, rows + 4, vecs, ny), jnp.float32)
    fetches = 4
    dma = pltpu.SemaphoreType.DMA
    filtered, corr, energy = pl.pallas_call(
        functools.partial(kernel, cells, slabs, poles),
        out_shape=(
            jax.ShapeDtypeStruct((planes, rows, vecs, ny), jnp.float32),
            jax.ShapeDtypeStruct((2, nb, nb), jnp.float32),
            jax.ShapeDtypeStruct((2, nb, nb), jnp.float32),
        ),
        in_specs=[whole, whole],
        out_specs=(vmem, vmem, vmem),
        scratch_shapes=[
            pltpu.VMEM(flat.shape, jnp.float32),
            pltpu.VMEM(potential.shape, jnp.float32),
            field,
            field,
            pltpu.VMEM((planes + 1, rows + 1, vecs, ny), jnp.float32),
            pltpu.VMEM((2, nx, ny), jnp.float32),
            field,
            pltpu.VMEM((8 * vecs, planes * rows * ny), jnp.bfloat16),
            pltpu.VMEM((2, vecs, ny), jnp.float32),
            pltpu.VMEM((slabs, vecs, ny), jnp.float32),
            pltpu.VMEM((poles, vecs, ny), jnp.float32),
            dma((fetches + 1,)),
            dma((8,)),
            dma((8,)),
            dma((slabs,)),
            dma((slabs,)),
            dma((poles,)),
            dma((poles,)),
        ],
        compiler_params=pltpu.CompilerParams(
            collective_id=0, has_side_effects=True, vmem_limit_bytes=63 * 1024 * 1024
        ),
    )(flat, potential)
    filtered = filtered.reshape(planes, rows, 2, nb, ny).transpose(2, 3, 0, 1, 4)
    return filtered, corr, energy


def solution(mesh):
    in_specs = (P(None, None, "slab", None, None), P("slab", None, None))
    out_specs = (P(None, None, "slab", "pole", None), P(), P())
    body = functools.partial(on_device, mesh.shape["slab"], mesh.shape["pole"])
    return jax.shard_map(
        body, mesh=mesh, in_specs=in_specs, out_specs=out_specs, check_vma=False
    )
```

```python
import functools
import math

import jax
import jax.numpy as jnp
from jax import lax
from jax.experimental import pallas as pl
from jax.experimental.pallas import tpu as pltpu
from jax.sharding import PartitionSpec as P

ITERS = 3
CENTER = 2.0
RADIUS = 1.5
BASE = 4.0

MESH = pl.DeviceIdType.MESH


def cmul(a, b):
    return (a[0] * b[0] - a[1] * b[1], a[0] * b[1] + a[1] * b[0])


def cmul_conj(a, b):
    return (a[0] * b[0] + a[1] * b[1], a[0] * b[1] - a[1] * b[0])


def cadd(a, b):
    return (a[0] + b[0], a[1] + b[1])


def csub(a, b):
    return (a[0] - b[0], a[1] - b[1])


def cdiv(n, d):
    inv = 1.0 / (d[0] * d[0] + d[1] * d[1])
    return ((n[0] * d[0] + n[1] * d[1]) * inv, (n[1] * d[0] - n[0] * d[1]) * inv)


def cocg_coefficients(moments, shift):
    def form(a, b):
        anti = {}
        for i, ai in enumerate(a):
            for j, bj in enumerate(b):
                term = bj if ai is None else cmul(ai, bj)
                anti[i + j] = cadd(anti[i + j], term) if i + j in anti else term
        total = None
        for n, coef in anti.items():
            term = cmul(coef, moments[n])
            total = term if total is None else cadd(total, term)
        return total

    one = (jnp.ones_like(shift[0]), jnp.zeros_like(shift[0]))
    x = []
    r = [one]
    p = [one]
    rho = moments[0]
    for iteration in range(ITERS):
        q = [cmul(shift, c) for c in p] + [None]
        for i, c in enumerate(p):
            q[i + 1] = (-c[0], -c[1]) if q[i + 1] is None else csub(q[i + 1], c)
        alpha = cdiv(rho, form(p, q))
        step = [cmul(alpha, c) for c in p]
        x = [cadd(x[i], c) if i < len(x) else c for i, c in enumerate(step)]
        if iteration + 1 < ITERS:
            down = [cmul(alpha, c) for c in q]
            r = [csub(r[i], c) if i < len(r) else (-c[0], -c[1]) for i, c in enumerate(down)]
            rho_new = form(r, r)
            beta = cdiv(rho_new, rho)
            p = [cadd(c, cmul(beta, p[i])) if i < len(p) else c for i, c in enumerate(r)]
            rho = rho_new
    return x


def gather_kernel(
    slabs, poles, v_hbm, pot_hbm, basis_hbm, packed_ref,
    v_ref, pot_ref, e0, e1, e2, pot_halo, diag, stack, last, payload, from_slab, from_pole,
    fetch, store, halo_send, halo_recv, slab_send, slab_recv, pole_send, pole_recv,
):
    planes, nx, lanes = pot_ref.shape
    vecs = e0.shape[2]
    nb = vecs // 2
    rows = basis_hbm.shape[2]
    slab = lax.axis_index("slab")
    pole = lax.axis_index("pole")
    x0 = pole * rows
    up = lax.rem(slab + 1, slabs)
    down = lax.rem(slab + slabs - 1, slabs)
    ahead = lax.rem(pole + 1, poles)
    back = lax.rem(pole + poles - 1, poles)

    order = [0, planes - 1] + list(range(1, planes - 1))
    fetches = {
        z: pltpu.make_async_copy(v_hbm.at[:, z], v_ref.at[z], fetch.at[z]) for z in order
    }
    fetch_pot = pltpu.make_async_copy(pot_hbm, pot_ref, fetch.at[planes])
    for z in order:
        fetches[z].start()
    fetch_pot.start()

    barrier = pltpu.get_barrier_semaphore()
    for d in range(1, slabs):
        pl.semaphore_signal(
            barrier, inc=1, device_id={"slab": lax.rem(slab + d, slabs)}, device_id_type=MESH
        )
    for d in range(1, poles):
        pl.semaphore_signal(
            barrier, inc=1, device_id={"pole": lax.rem(pole + d, poles)}, device_id_type=MESH
        )
    empty = jnp.zeros((vecs, stack.shape[1]), stack.dtype)
    stack[pl.ds(3 * vecs, vecs)] = empty
    stack[pl.ds(7 * vecs, vecs)] = empty

    def window(q):
        return lax.rem(x0 + (q - 2 + nx), nx)

    lines = v_ref.reshape(planes * vecs * nx, lanes)

    def gather(z):
        fetches[z].wait()
        for q in range(rows + 4):
            e0[z + 2, q] = lines[pl.ds(z * vecs * nx + window(q), vecs, stride=nx), :]

    copies = []

    def send(i, src, dst, axis, target):
        copy = pltpu.make_async_remote_copy(
            src_ref=src, dst_ref=dst, send_sem=halo_send.at[i], recv_sem=halo_recv.at[i],
            device_id={axis: target}, device_id_type=MESH,
        )
        copy.start()
        copies.append(copy)
        return copy

    own = pl.ds(2, rows)

    def send_plane(i, z, there, target):
        return send(i, e0.at[z + 2, own], e0.at[there + 2, own], "slab", target)

    gather(0)
    gather(planes - 1)
    fetch_pot.wait()
    pl.semaphore_wait(barrier, slabs - 1 + poles - 1)
    near = [
        send_plane(2, planes - 1, -1, up),
        send_plane(3, 0, planes, down),
        send(0, pot_ref.at[planes - 1], pot_halo.at[0], "slab", up),
        send(1, pot_ref.at[0], pot_halo.at[1], "slab", down),
    ]
    for z in range(1, planes - 1):
        gather(z)
    far = [
        send_plane(4, planes - 2, -2, up),
        send_plane(5, 1, planes + 1, down),
    ]

    def spread(ref, z, p):
        for q in range(1, rows + 3):
            line = ref[z, pl.ds(window(q), 1), :] + (3.0 - BASE)
            diag[p, q] = jnp.broadcast_to(line, (vecs, lanes))

    def roll_y(block, by):
        flat = block.reshape(block.shape[0] * vecs, lanes)
        return pltpu.roll(flat, by, 1).reshape(block.shape)

    def apply(src, z, lo, hi):
        p = z + 2
        here = src[p, lo:hi]
        beside = src[p - 1, lo:hi] + src[p + 1, lo:hi]
        beside = beside + src[p, lo - 1:hi - 1] + src[p, lo + 1:hi + 1]
        beside = beside + (roll_y(here, 1) + roll_y(here, lanes - 1))
        return diag[p, lo:hi] * here - 0.5 * beside

    def first_power(z, lo=2, hi=rows + 2):
        e1[z + 2, lo:hi] = apply(e0, z, lo, hi)

    def second_power(z):
        e2[z, :rows] = apply(e1, z, 2, rows + 2)

    for z in range(planes):
        spread(pot_ref, z, z + 2)
    for z in range(1, planes - 1):
        first_power(z, 1, rows + 3)
    for copy in near:
        copy.wait_recv()
    sides = []
    for i, p in ((6, 1), (8, planes + 2)):
        sides.append(send(i, e0.at[p, 2], e0.at[p, rows + 2], "pole", back))
        sides.append(send(i + 1, e0.at[p, rows + 1], e0.at[p, 1], "pole", ahead))
    first_power(0)
    first_power(planes - 1)
    spread(pot_halo, 0, 1)
    spread(pot_halo, 1, planes + 2)
    for z in range(1, planes - 1):
        second_power(z)
    for copy in sides:
        copy.wait_recv()
    for z in (0, planes - 1):
        first_power(z, 1, 2)
        first_power(z, rows + 2, rows + 3)
    for copy in far:
        copy.wait_recv()
    first_power(-1)
    first_power(planes)
    second_power(0)
    edge = [send(10, e2.at[0, pl.ds(0, rows)], e2.at[planes, pl.ds(0, rows)], "slab", down)]
    second_power(planes - 1)
    edge.append(send(11, e2.at[pl.ds(0, planes), 0], e2.at[pl.ds(0, planes), rows], "pole", back))
    stores = [
        pltpu.make_async_copy(src, basis_hbm.at[k], store.at[k])
        for k, src in enumerate((
            e0.at[pl.ds(2, planes), own],
            e1.at[pl.ds(2, planes), own],
            e2.at[pl.ds(0, planes), pl.ds(0, rows)],
        ))
    ]
    for copy in stores:
        copy.start()

    lo, hi = 2, rows + 2
    sums = [None] * 12

    def split(into, high_row, low_row, z, u):
        high = u.astype(jnp.bfloat16)
        low = (u - high.astype(jnp.float32)).astype(jnp.bfloat16)
        for r in range(rows):
            at = pl.ds((z * rows + r) * lanes, lanes)
            into[pl.ds(high_row, vecs), at] = high[r]
            into[pl.ds(low_row, vecs), at] = low[r]

    def collect(n, a, b):
        re = a[:, :nb] * b[:, :nb] - a[:, nb:] * b[:, nb:]
        im = a[:, :nb] * b[:, nb:] + a[:, nb:] * b[:, :nb]
        for i, value in ((n, jnp.sum(re, axis=0)), (6 + n, jnp.sum(im, axis=0))):
            sums[i] = value if sums[i] is None else sums[i] + value

    def products(a, b):
        full = lax.dot_general(
            a, b, (((1,), (1,)), ((), ())), preferred_element_type=jnp.float32
        )
        h = full.shape[0] // 2
        return full[:h, :h] + (full[:h, h:] + full[h:, :h] + full[h:, h:])

    for z in range(planes):
        u0, u1, u2 = e0[z + 2, lo:hi], e1[z + 2, lo:hi], e2[z, :rows]
        for k, u in enumerate((u0, u1, u2)):
            split(stack, k * vecs, (4 + k) * vecs, z, u)
        for n, (a, b) in enumerate(((u0, u0), (u0, u1), (u1, u1), (u1, u2), (u2, u2))):
            collect(n, a, b)
    s = products(stack[...], stack[...])

    lane = lax.broadcasted_iota(jnp.int32, (nb, lanes), 1)
    row = lax.broadcasted_iota(jnp.int32, (nb, lanes), 0)
    to_left = lanes - nb

    def parts(block):
        re, im = block[:nb], block[nb:]
        return re + pltpu.roll(im, to_left, 1), pltpu.roll(re, to_left, 1) - im

    packed = []
    for k in range(3):
        re, im = parts(s[k * vecs:(k + 1) * vecs])
        packed.append(jnp.where(row <= lax.rem(lane, vecs), re, im))
    pieces = [
        packed[0], pltpu.roll(packed[0], to_left, 1),
        packed[1], pltpu.roll(packed[1], to_left, 1), packed[2],
    ]
    for copy in edge:
        copy.wait_recv()
    for z in range(planes):
        u2 = e2[z, :rows]
        beside = e2[z + 1, :rows] + e2[z, 1:rows + 1] + roll_y(u2, lanes - 1)
        y = 0.5 * (diag[z + 2, lo:hi] * u2 - beside)
        split(last, 0, vecs, z, y)
        collect(5, u2, y)
    second = jnp.concatenate(
        [stack[pl.ds(2 * vecs, vecs)], stack[pl.ds(6 * vecs, vecs)]], axis=0
    )
    m = products(second, last[...])
    m = jnp.concatenate([m, jnp.zeros((vecs, lanes - vecs), jnp.float32)], axis=1)
    re, im = parts(m)
    pieces += [pltpu.roll(re, 5 * nb, 1), pltpu.roll(im, 6 * nb, 1)]
    out = pieces[0]
    for n in range(1, 7):
        out = jnp.where(lane >= n * nb, pieces[n], out)
    for n in range(12):
        value = jnp.sum(sums[n], axis=1, keepdims=True)
        out = jnp.where(lane == 7 * nb + n, value * (2.0 if n in (5, 11) else 1.0), out)
    payload[0] = out

    def exchange(source, landing, axis, count, me, send_sem, recv_sem):
        sent = []
        for d in range(1, count):
            copy = pltpu.make_async_remote_copy(
                src_ref=source, dst_ref=landing.at[me], send_sem=send_sem.at[d],
                recv_sem=recv_sem.at[d], device_id={axis: lax.rem(me + d, count)},
                device_id_type=MESH,
            )
            copy.start()
            sent.append(copy)
        landing[me] = source[...]
        for copy in sent:
            copy.wait_recv()
        total = landing[0]
        for i in range(1, count):
            total = total + landing[i]
        return total, sent

    total, sent = exchange(payload.at[0], from_slab, "slab", slabs, slab, slab_send, slab_recv)
    copies += sent
    payload[1] = total
    total, sent = exchange(payload.at[1], from_pole, "pole", poles, pole, pole_send, pole_recv)
    copies += sent
    packed_ref[...] = total
    for copy in copies:
        copy.wait_send()
    for copy in stores:
        copy.wait()


def filter_kernel(cells, poles, basis_hbm, packed_ref, f_ref, corr_ref, en_ref, basis, fetch):
    _, planes, rows, vecs, lanes = basis.shape
    nb = vecs // 2
    bring = pltpu.make_async_copy(basis_hbm, basis, fetch)
    bring.start()
    packed = packed_ref[...]
    lane = lax.broadcasted_iota(jnp.int32, (nb, lanes), 1)
    row = lax.broadcasted_iota(jnp.int32, (nb, lanes), 0)

    def column(n):
        at = 7 * nb + n
        return jnp.broadcast_to(packed[:, at:at + 1], (nb, lanes))

    moments = [(column(n), column(6 + n)) for n in range(6)]
    shift_re = jnp.zeros((nb, lanes), jnp.float32)
    shift_im, weight_re, weight_im = shift_re, shift_re, shift_re
    for j in range(poles):
        theta = 2.0 * math.pi / poles * (j + 0.5)
        c, t = math.cos(theta), math.sin(theta)
        here = lane >= 0 if j == 0 else lane == j
        shift_re = jnp.where(here, CENTER - BASE + RADIUS * c, shift_re)
        shift_im = jnp.where(here, RADIUS * t, shift_im)
        weight_re = jnp.where(lane == j, RADIUS * c / poles, weight_re)
        weight_im = jnp.where(lane == j, RADIUS * t / poles, weight_im)
    coefs = []
    for x in cocg_coefficients(moments, (shift_re, shift_im)):
        x = cmul((weight_re, weight_im), x)
        coefs.append(
            tuple(jnp.broadcast_to(jnp.sum(c, axis=1, keepdims=True), (nb, lanes)) for c in x)
        )

    bring.wait()
    for z in range(planes):
        re = im = None
        for (cr, ci), u in zip(coefs, (basis[0, z], basis[1, z], basis[2, z])):
            ur, ui = u[:, :nb], u[:, nb:]
            tr, ti = cr * ur - ci * ui, cr * ui + ci * ur
            re, im = (tr, ti) if re is None else (re + tr, im + ti)
        for r in range(rows):
            both = jnp.concatenate([re[r], im[r]], axis=0)
            f_ref[pl.ds(z * rows + r, vecs, stride=planes * rows), :] = both

    square = jnp.concatenate([packed, jnp.zeros((lanes - nb, lanes), jnp.float32)], axis=0)
    turned = jnp.transpose(square)

    def piece(n):
        here = packed if n == 0 else pltpu.roll(packed, lanes - n * nb, 1)
        return here, turned[n * nb:(n + 1) * nb]

    grams = []
    for n in range(5):
        here, across = piece(n)
        re = jnp.where(row <= lane, here, across)
        im = jnp.where(row > lane, here, jnp.where(row < lane, -across, 0.0))
        grams.append((re, im))
    (re, re_t), (im, im_t) = piece(5), piece(6)
    grams.append((re + re_t, im - im_t))
    across = [
        tuple(jnp.sum(jnp.where(lane == row, c, 0.0), axis=0, keepdims=True) for c in coef)
        for coef in coefs
    ]

    def quadratic(first_power):
        out = None
        for l in range(3):
            term = None
            for k in range(3):
                t = cmul_conj(coefs[k], grams[k + l + first_power])
                term = t if term is None else cadd(term, t)
            term = cmul(term, across[l])
            out = term if out is None else cadd(out, term)
        return out

    corr = quadratic(0)
    energy = quadratic(1)
    for i in range(2):
        corr_ref[i] = (corr[i] / cells)[:, :nb]
        en_ref[i] = ((energy[i] + BASE * corr[i]) / cells)[:, :nb]


def on_device(slabs, poles, vectors, potential):
    _, nb, planes, nx, ny = vectors.shape
    rows = nx // poles
    vecs = 2 * nb
    cells = float(planes * slabs * nx * ny)
    vmem = pl.BlockSpec(memory_space=pltpu.VMEM)
    whole = pl.BlockSpec(memory_space=pl.ANY)
    dma = pltpu.SemaphoreType.DMA
    scratch = lambda *shape: pltpu.VMEM(shape, jnp.float32)
    limit = 63 * 1024 * 1024
    basis, packed = pl.pallas_call(
        functools.partial(gather_kernel, slabs, poles),
        out_shape=(
            jax.ShapeDtypeStruct((3, planes, rows, vecs, ny), jnp.float32),
            jax.ShapeDtypeStruct((nb, ny), jnp.float32),
        ),
        in_specs=[whole, whole],
        out_specs=(whole, vmem),
        scratch_shapes=[
            scratch(planes, vecs, nx, ny),
            scratch(planes, nx, ny),
            scratch(planes + 4, rows + 4, vecs, ny),
            scratch(planes + 4, rows + 4, vecs, ny),
            scratch(planes + 1, rows + 1, vecs, ny),
            scratch(2, nx, ny),
            scratch(planes + 4, rows + 4, vecs, ny),
            pltpu.VMEM((8 * vecs, planes * rows * ny), jnp.bfloat16),
            pltpu.VMEM((2 * vecs, planes * rows * ny), jnp.bfloat16),
            scratch(2, nb, ny),
            scratch(slabs, nb, ny),
            scratch(poles, nb, ny),
            dma((planes + 1,)),
            dma((3,)),
            dma((12,)),
            dma((12,)),
            dma((slabs,)),
            dma((slabs,)),
            dma((poles,)),
            dma((poles,)),
        ],
        compiler_params=pltpu.CompilerParams(
            collective_id=0, has_side_effects=True, vmem_limit_bytes=limit
        ),
    )(vectors.reshape(vecs, planes, nx, ny), potential)
    filtered, corr, energy = pl.pallas_call(
        functools.partial(filter_kernel, cells, poles),
        out_shape=(
            jax.ShapeDtypeStruct((vecs * planes * rows, ny), jnp.float32),
            jax.ShapeDtypeStruct((2, nb, nb), jnp.float32),
            jax.ShapeDtypeStruct((2, nb, nb), jnp.float32),
        ),
        in_specs=[whole, vmem],
        out_specs=(vmem, vmem, vmem),
        scratch_shapes=[scratch(3, planes, rows, vecs, ny), dma],
        compiler_params=pltpu.CompilerParams(vmem_limit_bytes=limit),
    )(basis, packed)
    return filtered.reshape(2, nb, planes, rows, ny), corr, energy


def solution(mesh):
    in_specs = (P(None, None, "slab", None, None), P("slab", None, None))
    out_specs = (P(None, None, "slab", "pole", None), P(), P())
    body = functools.partial(on_device, mesh.shape["slab"], mesh.shape["pole"])
    return jax.shard_map(
        body, mesh=mesh, in_specs=in_specs, out_specs=out_specs, check_vma=False
    )
```

```python
import functools
import math

import jax
import jax.numpy as jnp
from jax import lax
from jax.experimental import pallas as pl
from jax.experimental.pallas import tpu as pltpu
from jax.sharding import PartitionSpec as P

ITERS = 3
CENTER = 2.0
RADIUS = 1.5
BASE = 4.0

MESH = pl.DeviceIdType.MESH


def cmul(a, b):
    return (a[0] * b[0] - a[1] * b[1], a[0] * b[1] + a[1] * b[0])


def cmul_conj(a, b):
    return (a[0] * b[0] + a[1] * b[1], a[0] * b[1] - a[1] * b[0])


def cadd(a, b):
    return (a[0] + b[0], a[1] + b[1])


def csub(a, b):
    return (a[0] - b[0], a[1] - b[1])


def cdiv(n, d):
    inv = 1.0 / (d[0] * d[0] + d[1] * d[1])
    return ((n[0] * d[0] + n[1] * d[1]) * inv, (n[1] * d[0] - n[0] * d[1]) * inv)


def cocg_coefficients(moments, shift):
    def form(a, b):
        anti = {}
        for i, ai in enumerate(a):
            for j, bj in enumerate(b):
                term = bj if ai is None else cmul(ai, bj)
                anti[i + j] = cadd(anti[i + j], term) if i + j in anti else term
        total = None
        for n, coef in anti.items():
            term = cmul(coef, moments[n])
            total = term if total is None else cadd(total, term)
        return total

    one = (jnp.ones_like(shift[0]), jnp.zeros_like(shift[0]))
    x = []
    r = [one]
    p = [one]
    rho = moments[0]
    for iteration in range(ITERS):
        q = [cmul(shift, c) for c in p] + [None]
        for i, c in enumerate(p):
            q[i + 1] = (-c[0], -c[1]) if q[i + 1] is None else csub(q[i + 1], c)
        alpha = cdiv(rho, form(p, q))
        step = [cmul(alpha, c) for c in p]
        x = [cadd(x[i], c) if i < len(x) else c for i, c in enumerate(step)]
        if iteration + 1 < ITERS:
            down = [cmul(alpha, c) for c in q]
            r = [csub(r[i], c) if i < len(r) else (-c[0], -c[1]) for i, c in enumerate(down)]
            rho_new = form(r, r)
            beta = cdiv(rho_new, rho)
            p = [cadd(c, cmul(beta, p[i])) if i < len(p) else c for i, c in enumerate(r)]
            rho = rho_new
    return x


def gather_kernel(
    slabs, poles, v_hbm, pot_hbm, basis_hbm, packed_ref,
    v_ref, pot_ref, e0, e1, e2, pot_halo, diag, stack, last, payload, from_slab, from_pole,
    fetch, store, halo_send, halo_recv, slab_send, slab_recv, pole_send, pole_recv,
):
    planes, nx, lanes = pot_ref.shape
    vecs = e0.shape[2]
    nb = vecs // 2
    rows = basis_hbm.shape[2]
    slab = lax.axis_index("slab")
    pole = lax.axis_index("pole")
    x0 = pole * rows
    up = lax.rem(slab + 1, slabs)
    down = lax.rem(slab + slabs - 1, slabs)

    order = [0, planes - 1] + list(range(1, planes - 1))
    fetches = {
        z: pltpu.make_async_copy(v_hbm.at[:, z], v_ref.at[z], fetch.at[z]) for z in order
    }
    fetch_pot = pltpu.make_async_copy(pot_hbm, pot_ref, fetch.at[planes])
    for z in order:
        fetches[z].start()
    fetch_pot.start()

    barrier = pltpu.get_barrier_semaphore()
    for d in range(1, slabs):
        pl.semaphore_signal(
            barrier, inc=1, device_id={"slab": lax.rem(slab + d, slabs)}, device_id_type=MESH
        )
    for d in range(1, poles):
        pl.semaphore_signal(
            barrier, inc=1, device_id={"pole": lax.rem(pole + d, poles)}, device_id_type=MESH
        )
    empty = jnp.zeros((vecs, stack.shape[1]), stack.dtype)
    stack[pl.ds(3 * vecs, vecs)] = empty
    stack[pl.ds(7 * vecs, vecs)] = empty

    def window(q):
        return lax.rem(x0 + (q - 2 + nx), nx)

    lines = v_ref.reshape(planes * vecs * nx, lanes)

    def gather(z):
        fetches[z].wait()
        for q in range(rows + 5):
            e0[z + 2, q] = lines[pl.ds(z * vecs * nx + window(q), vecs, stride=nx), :]

    copies = []

    def send(i, src, dst, axis, target):
        copy = pltpu.make_async_remote_copy(
            src_ref=src, dst_ref=dst, send_sem=halo_send.at[i], recv_sem=halo_recv.at[i],
            device_id={axis: target}, device_id_type=MESH,
        )
        copy.start()
        copies.append(copy)
        return copy

    own = pl.ds(2, rows)

    def send_plane(i, z, there, lo, hi, target):
        at = pl.ds(lo, hi - lo)
        return send(i, e0.at[z + 2, at], e0.at[there + 2, at], "slab", target)

    gather(0)
    gather(planes - 1)
    fetch_pot.wait()
    pl.semaphore_wait(barrier, slabs - 1 + poles - 1)
    near = [
        send_plane(2, planes - 1, -1, 1, rows + 4, up),
        send_plane(3, 0, planes, 0, rows + 4, down),
        send(0, pot_ref.at[planes - 1], pot_halo.at[0], "slab", up),
        send(1, pot_ref.at[pl.ds(0, 2)], pot_halo.at[pl.ds(1, 2)], "slab", down),
    ]
    gather(1)
    far = [send_plane(4, 1, planes + 1, 1, rows + 3, down)]
    for z in range(2, planes - 1):
        gather(z)
    far.append(send_plane(5, planes - 2, -2, 2, rows + 3, up))
    farthest = send_plane(6, 2, planes + 2, 2, rows + 2, down)

    def spread(ref, z, p):
        for q in range(1, rows + 4):
            line = ref[z, pl.ds(window(q), 1), :] + (3.0 - BASE)
            diag[p, q] = jnp.broadcast_to(line, (vecs, lanes))

    def roll_y(block, by):
        flat = block.reshape(block.shape[0] * vecs, lanes)
        return pltpu.roll(flat, by, 1).reshape(block.shape)

    def apply(src, z, lo, hi):
        p = z + 2
        here = src[p, lo:hi]
        beside = src[p - 1, lo:hi] + src[p + 1, lo:hi]
        beside = beside + src[p, lo - 1:hi - 1] + src[p, lo + 1:hi + 1]
        beside = beside + (roll_y(here, 1) + roll_y(here, lanes - 1))
        return diag[p, lo:hi] * here - 0.5 * beside

    def first_power(z, lo=2, hi=rows + 2):
        e1[z + 2, lo:hi] = apply(e0, z, lo, hi)

    def second_power(z, lo=2, hi=rows + 3):
        e2[z, lo - 2:hi - 2] = apply(e1, z, lo, hi)

    for z in range(planes):
        spread(pot_ref, z, z + 2)
    for z in range(1, planes - 1):
        first_power(z, 1, rows + 4)
    for copy in near:
        copy.wait_recv()
    first_power(0, 1, rows + 4)
    first_power(planes - 1, 1, rows + 4)
    spread(pot_halo, 0, 1)
    spread(pot_halo, 1, planes + 2)
    spread(pot_halo, 2, planes + 3)
    for z in range(1, planes - 1):
        second_power(z)
    for copy in far:
        copy.wait_recv()
    first_power(-1, 2, rows + 3)
    first_power(planes, 1, rows + 3)
    second_power(0)
    second_power(planes - 1)
    stores = [
        pltpu.make_async_copy(src, basis_hbm.at[k], store.at[k])
        for k, src in enumerate((
            e0.at[pl.ds(2, planes), own],
            e1.at[pl.ds(2, planes), own],
            e2.at[pl.ds(0, planes), pl.ds(0, rows)],
        ))
    ]
    for copy in stores:
        copy.start()

    lo, hi = 2, rows + 2
    sums = [None] * 12

    def split(into, high_row, low_row, z, u):
        high = u.astype(jnp.bfloat16)
        low = (u - high.astype(jnp.float32)).astype(jnp.bfloat16)
        for r in range(rows):
            at = pl.ds((z * rows + r) * lanes, lanes)
            into[pl.ds(high_row, vecs), at] = high[r]
            into[pl.ds(low_row, vecs), at] = low[r]

    def collect(n, a, b):
        re = a[:, :nb] * b[:, :nb] - a[:, nb:] * b[:, nb:]
        im = a[:, :nb] * b[:, nb:] + a[:, nb:] * b[:, :nb]
        for i, value in ((n, jnp.sum(re, axis=0)), (6 + n, jnp.sum(im, axis=0))):
            sums[i] = value if sums[i] is None else sums[i] + value

    def products(a, b):
        full = lax.dot_general(
            a, b, (((1,), (1,)), ((), ())), preferred_element_type=jnp.float32
        )
        h = full.shape[0] // 2
        return full[:h, :h] + (full[:h, h:] + full[h:, :h] + full[h:, h:])

    for z in range(planes):
        u0, u1, u2 = e0[z + 2, lo:hi], e1[z + 2, lo:hi], e2[z, :rows]
        for k, u in enumerate((u0, u1, u2)):
            split(stack, k * vecs, (4 + k) * vecs, z, u)
        for n, (a, b) in enumerate(((u0, u0), (u0, u1), (u1, u1), (u1, u2), (u2, u2))):
            collect(n, a, b)
    s = products(stack[...], stack[...])

    lane = lax.broadcasted_iota(jnp.int32, (nb, lanes), 1)
    row = lax.broadcasted_iota(jnp.int32, (nb, lanes), 0)
    to_left = lanes - nb

    def parts(block):
        re, im = block[:nb], block[nb:]
        return re + pltpu.roll(im, to_left, 1), pltpu.roll(re, to_left, 1) - im

    packed = []
    for k in range(3):
        re, im = parts(s[k * vecs:(k + 1) * vecs])
        packed.append(jnp.where(row <= lax.rem(lane, vecs), re, im))
    pieces = [
        packed[0], pltpu.roll(packed[0], to_left, 1),
        packed[1], pltpu.roll(packed[1], to_left, 1), packed[2],
    ]
    farthest.wait_recv()
    first_power(planes + 1)
    second_power(planes, 2, rows + 2)
    for z in range(planes):
        u2 = e2[z, :rows]
        beside = e2[z + 1, :rows] + e2[z, 1:rows + 1] + roll_y(u2, lanes - 1)
        y = 0.5 * (diag[z + 2, lo:hi] * u2 - beside)
        split(last, 0, vecs, z, y)
        collect(5, u2, y)
    second = jnp.concatenate(
        [stack[pl.ds(2 * vecs, vecs)], stack[pl.ds(6 * vecs, vecs)]], axis=0
    )
    m = products(second, last[...])
    m = jnp.concatenate([m, jnp.zeros((vecs, lanes - vecs), jnp.float32)], axis=1)
    re, im = parts(m)
    pieces += [pltpu.roll(re, 5 * nb, 1), pltpu.roll(im, 6 * nb, 1)]
    out = pieces[0]
    for n in range(1, 7):
        out = jnp.where(lane >= n * nb, pieces[n], out)
    for n in range(12):
        value = jnp.sum(sums[n], axis=1, keepdims=True)
        out = jnp.where(lane == 7 * nb + n, value * (2.0 if n in (5, 11) else 1.0), out)
    payload[0] = out

    def exchange(source, landing, axis, count, me, send_sem, recv_sem):
        sent = []
        for d in range(1, count):
            copy = pltpu.make_async_remote_copy(
                src_ref=source, dst_ref=landing.at[me], send_sem=send_sem.at[d],
                recv_sem=recv_sem.at[d], device_id={axis: lax.rem(me + d, count)},
                device_id_type=MESH,
            )
            copy.start()
            sent.append(copy)
        landing[me] = source[...]
        for copy in sent:
            copy.wait_recv()
        total = landing[0]
        for i in range(1, count):
            total = total + landing[i]
        return total, sent

    total, sent = exchange(payload.at[0], from_slab, "slab", slabs, slab, slab_send, slab_recv)
    copies += sent
    payload[1] = total
    total, sent = exchange(payload.at[1], from_pole, "pole", poles, pole, pole_send, pole_recv)
    copies += sent
    packed_ref[...] = total
    for copy in copies:
        copy.wait_send()
    for copy in stores:
        copy.wait()


def filter_kernel(cells, poles, basis_hbm, packed_ref, f_ref, corr_ref, en_ref, basis, fetch):
    _, planes, rows, vecs, lanes = basis.shape
    nb = vecs // 2
    bring = pltpu.make_async_copy(basis_hbm, basis, fetch)
    bring.start()
    packed = packed_ref[...]
    lane = lax.broadcasted_iota(jnp.int32, (nb, lanes), 1)
    row = lax.broadcasted_iota(jnp.int32, (nb, lanes), 0)

    def column(n):
        at = 7 * nb + n
        return jnp.broadcast_to(packed[:, at:at + 1], (nb, lanes))

    moments = [(column(n), column(6 + n)) for n in range(6)]
    shift_re = jnp.zeros((nb, lanes), jnp.float32)
    shift_im, weight_re, weight_im = shift_re, shift_re, shift_re
    for j in range(poles):
        theta = 2.0 * math.pi / poles * (j + 0.5)
        c, t = math.cos(theta), math.sin(theta)
        here = lane >= 0 if j == 0 else lane == j
        shift_re = jnp.where(here, CENTER - BASE + RADIUS * c, shift_re)
        shift_im = jnp.where(here, RADIUS * t, shift_im)
        weight_re = jnp.where(lane == j, RADIUS * c / poles, weight_re)
        weight_im = jnp.where(lane == j, RADIUS * t / poles, weight_im)
    coefs = []
    for x in cocg_coefficients(moments, (shift_re, shift_im)):
        x = cmul((weight_re, weight_im), x)
        coefs.append(
            tuple(jnp.broadcast_to(jnp.sum(c, axis=1, keepdims=True), (nb, lanes)) for c in x)
        )

    bring.wait()
    for z in range(planes):
        re = im = None
        for (cr, ci), u in zip(coefs, (basis[0, z], basis[1, z], basis[2, z])):
            ur, ui = u[:, :nb], u[:, nb:]
            tr, ti = cr * ur - ci * ui, cr * ui + ci * ur
            re, im = (tr, ti) if re is None else (re + tr, im + ti)
        for r in range(rows):
            both = jnp.concatenate([re[r], im[r]], axis=0)
            f_ref[pl.ds(z * rows + r, vecs, stride=planes * rows), :] = both

    square = jnp.concatenate([packed, jnp.zeros((lanes - nb, lanes), jnp.float32)], axis=0)
    turned = jnp.transpose(square)

    def piece(n):
        here = packed if n == 0 else pltpu.roll(packed, lanes - n * nb, 1)
        return here, turned[n * nb:(n + 1) * nb]

    grams = []
    for n in range(5):
        here, across = piece(n)
        re = jnp.where(row <= lane, here, across)
        im = jnp.where(row > lane, here, jnp.where(row < lane, -across, 0.0))
        grams.append((re, im))
    (re, re_t), (im, im_t) = piece(5), piece(6)
    grams.append((re + re_t, im - im_t))
    across = [
        tuple(jnp.sum(jnp.where(lane == row, c, 0.0), axis=0, keepdims=True) for c in coef)
        for coef in coefs
    ]

    def quadratic(first_power):
        out = None
        for l in range(3):
            term = None
            for k in range(3):
                t = cmul_conj(coefs[k], grams[k + l + first_power])
                term = t if term is None else cadd(term, t)
            term = cmul(term, across[l])
            out = term if out is None else cadd(out, term)
        return out

    corr = quadratic(0)
    energy = quadratic(1)
    for i in range(2):
        corr_ref[i] = (corr[i] / cells)[:, :nb]
        en_ref[i] = ((energy[i] + BASE * corr[i]) / cells)[:, :nb]


def on_device(slabs, poles, vectors, potential):
    _, nb, planes, nx, ny = vectors.shape
    rows = nx // poles
    vecs = 2 * nb
    cells = float(planes * slabs * nx * ny)
    vmem = pl.BlockSpec(memory_space=pltpu.VMEM)
    whole = pl.BlockSpec(memory_space=pl.ANY)
    dma = pltpu.SemaphoreType.DMA
    scratch = lambda *shape: pltpu.VMEM(shape, jnp.float32)
    limit = 63 * 1024 * 1024
    basis, packed = pl.pallas_call(
        functools.partial(gather_kernel, slabs, poles),
        out_shape=(
            jax.ShapeDtypeStruct((3, planes, rows, vecs, ny), jnp.float32),
            jax.ShapeDtypeStruct((nb, ny), jnp.float32),
        ),
        in_specs=[whole, whole],
        out_specs=(whole, vmem),
        scratch_shapes=[
            scratch(planes, vecs, nx, ny),
            scratch(planes, nx, ny),
            scratch(planes + 5, rows + 5, vecs, ny),
            scratch(planes + 4, rows + 5, vecs, ny),
            scratch(planes + 1, rows + 1, vecs, ny),
            scratch(3, nx, ny),
            scratch(planes + 4, rows + 5, vecs, ny),
            pltpu.VMEM((8 * vecs, planes * rows * ny), jnp.bfloat16),
            pltpu.VMEM((2 * vecs, planes * rows * ny), jnp.bfloat16),
            scratch(2, nb, ny),
            scratch(slabs, nb, ny),
            scratch(poles, nb, ny),
            dma((planes + 1,)),
            dma((3,)),
            dma((7,)),
            dma((7,)),
            dma((slabs,)),
            dma((slabs,)),
            dma((poles,)),
            dma((poles,)),
        ],
        compiler_params=pltpu.CompilerParams(
            collective_id=0, has_side_effects=True, vmem_limit_bytes=limit
        ),
    )(vectors.reshape(vecs, planes, nx, ny), potential)
    filtered, corr, energy = pl.pallas_call(
        functools.partial(filter_kernel, cells, poles),
        out_shape=(
            jax.ShapeDtypeStruct((vecs * planes * rows, ny), jnp.float32),
            jax.ShapeDtypeStruct((2, nb, nb), jnp.float32),
            jax.ShapeDtypeStruct((2, nb, nb), jnp.float32),
        ),
        in_specs=[whole, vmem],
        out_specs=(vmem, vmem, vmem),
        scratch_shapes=[scratch(3, planes, rows, vecs, ny), dma],
        compiler_params=pltpu.CompilerParams(vmem_limit_bytes=limit),
    )(basis, packed)
    return filtered.reshape(2, nb, planes, rows, ny), corr, energy


def solution(mesh):
    in_specs = (P(None, None, "slab", None, None), P("slab", None, None))
    out_specs = (P(None, None, "slab", "pole", None), P(), P())
    body = functools.partial(on_device, mesh.shape["slab"], mesh.shape["pole"])
    return jax.shard_map(
        body, mesh=mesh, in_specs=in_specs, out_specs=out_specs, check_vma=False
    )
```

```python
import functools
import math

import jax
import jax.numpy as jnp
from jax import lax
from jax.experimental import pallas as pl
from jax.experimental.pallas import tpu as pltpu
from jax.sharding import PartitionSpec as P

ITERS = 3
CENTER = 2.0
RADIUS = 1.5
BASE = 4.0

MESH = pl.DeviceIdType.MESH


def cmul(a, b):
    return (a[0] * b[0] - a[1] * b[1], a[0] * b[1] + a[1] * b[0])


def cmul_conj(a, b):
    return (a[0] * b[0] + a[1] * b[1], a[0] * b[1] - a[1] * b[0])


def cadd(a, b):
    return (a[0] + b[0], a[1] + b[1])


def csub(a, b):
    return (a[0] - b[0], a[1] - b[1])


def cdiv(n, d):
    inv = 1.0 / (d[0] * d[0] + d[1] * d[1])
    return ((n[0] * d[0] + n[1] * d[1]) * inv, (n[1] * d[0] - n[0] * d[1]) * inv)


def cocg_coefficients(moments, shift):
    def form(a, b):
        anti = {}
        for i, ai in enumerate(a):
            for j, bj in enumerate(b):
                term = bj if ai is None else cmul(ai, bj)
                anti[i + j] = cadd(anti[i + j], term) if i + j in anti else term
        total = None
        for n, coef in anti.items():
            term = cmul(coef, moments[n])
            total = term if total is None else cadd(total, term)
        return total

    one = (jnp.ones_like(shift[0]), jnp.zeros_like(shift[0]))
    x = []
    r = [one]
    p = [one]
    rho = moments[0]
    for iteration in range(ITERS):
        q = [cmul(shift, c) for c in p] + [None]
        for i, c in enumerate(p):
            q[i + 1] = (-c[0], -c[1]) if q[i + 1] is None else csub(q[i + 1], c)
        alpha = cdiv(rho, form(p, q))
        step = [cmul(alpha, c) for c in p]
        x = [cadd(x[i], c) if i < len(x) else c for i, c in enumerate(step)]
        if iteration + 1 < ITERS:
            down = [cmul(alpha, c) for c in q]
            r = [csub(r[i], c) if i < len(r) else (-c[0], -c[1]) for i, c in enumerate(down)]
            rho_new = form(r, r)
            beta = cdiv(rho_new, rho)
            p = [cadd(c, cmul(beta, p[i])) if i < len(p) else c for i, c in enumerate(r)]
            rho = rho_new
    return x


def gather_kernel(
    slabs, poles, v_hbm, pot_hbm, basis_hbm, packed_ref,
    v_ref, pot_ref, e0, e1, e2, pot_halo, diag, stack, last, payload, from_slab, from_pole,
    fetch, store, halo_send, halo_recv, slab_send, slab_recv, pole_send, pole_recv,
):
    planes, nx, lanes = pot_ref.shape
    vecs = e0.shape[2]
    nb = vecs // 2
    rows = basis_hbm.shape[2]
    slab = lax.axis_index("slab")
    pole = lax.axis_index("pole")
    x0 = pole * rows
    up = lax.rem(slab + 1, slabs)
    down = lax.rem(slab + slabs - 1, slabs)

    order = [0, planes - 1] + list(range(1, planes - 1))
    fetches = {
        z: pltpu.make_async_copy(v_hbm.at[:, z], v_ref.at[z], fetch.at[z]) for z in order
    }
    fetch_pot = pltpu.make_async_copy(pot_hbm, pot_ref, fetch.at[planes])
    for z in order:
        fetches[z].start()
    fetch_pot.start()

    barrier = pltpu.get_barrier_semaphore()
    for d in range(1, slabs):
        pl.semaphore_signal(
            barrier, inc=1, device_id={"slab": lax.rem(slab + d, slabs)}, device_id_type=MESH
        )
    for d in range(1, poles):
        pl.semaphore_signal(
            barrier, inc=1, device_id={"pole": lax.rem(pole + d, poles)}, device_id_type=MESH
        )
    empty = jnp.zeros((vecs, stack.shape[1]), stack.dtype)
    stack[pl.ds(3 * vecs, vecs)] = empty
    stack[pl.ds(7 * vecs, vecs)] = empty

    def window(q):
        return lax.rem(x0 + (q - 2 + nx), nx)

    lines = v_ref.reshape(planes * vecs * nx, lanes)

    def gather(z):
        fetches[z].wait()
        for q in range(rows + 5):
            e0[z + 2, q] = lines[pl.ds(z * vecs * nx + window(q), vecs, stride=nx), :]

    copies = []

    def send(i, src, dst, axis, target):
        copy = pltpu.make_async_remote_copy(
            src_ref=src, dst_ref=dst, send_sem=halo_send.at[i], recv_sem=halo_recv.at[i],
            device_id={axis: target}, device_id_type=MESH,
        )
        copy.start()
        copies.append(copy)
        return copy

    own = pl.ds(2, rows)

    def send_plane(i, z, there, lo, hi, target):
        at = pl.ds(lo, hi - lo)
        return send(i, e0.at[z + 2, at], e0.at[there + 2, at], "slab", target)

    gather(0)
    gather(planes - 1)
    fetch_pot.wait()
    pl.semaphore_wait(barrier, slabs - 1 + poles - 1)
    near = [
        send_plane(2, planes - 1, -1, 1, rows + 4, up),
        send_plane(3, 0, planes, 0, rows + 4, down),
        send(0, pot_ref.at[planes - 1], pot_halo.at[0], "slab", up),
        send(1, pot_ref.at[pl.ds(0, 2)], pot_halo.at[pl.ds(1, 2)], "slab", down),
    ]
    gather(1)
    far = [send_plane(4, 1, planes + 1, 1, rows + 3, down)]
    for z in range(2, planes - 1):
        gather(z)
    far.append(send_plane(5, planes - 2, -2, 2, rows + 3, up))
    farthest = send_plane(6, 2, planes + 2, 2, rows + 2, down)

    def spread(ref, z, p):
        for q in range(1, rows + 4):
            line = ref[z, pl.ds(window(q), 1), :] + (3.0 - BASE)
            diag[p, q] = jnp.broadcast_to(line, (vecs, lanes))

    def roll_y(block, by):
        flat = block.reshape(block.shape[0] * vecs, lanes)
        return pltpu.roll(flat, by, 1).reshape(block.shape)

    def apply(src, z, lo, hi):
        p = z + 2
        here = src[p, lo:hi]
        beside = src[p - 1, lo:hi] + src[p + 1, lo:hi]
        beside = beside + src[p, lo - 1:hi - 1] + src[p, lo + 1:hi + 1]
        beside = beside + (roll_y(here, 1) + roll_y(here, lanes - 1))
        return diag[p, lo:hi] * here - 0.5 * beside

    def first_power(z, lo=2, hi=rows + 2):
        e1[z + 2, lo:hi] = apply(e0, z, lo, hi)

    def second_power(z, lo=2, hi=rows + 3):
        e2[z, lo - 2:hi - 2] = apply(e1, z, lo, hi)

    lo, hi = 2, rows + 2
    sums = [None] * 12
    inner, outer = range(1, planes - 1), (0, planes - 1)

    def split(into, high_row, low_row, z, u):
        high = u.astype(jnp.bfloat16)
        low = (u - high.astype(jnp.float32)).astype(jnp.bfloat16)
        for r in range(rows):
            at = pl.ds((z * rows + r) * lanes, lanes)
            into[pl.ds(high_row, vecs), at] = high[r]
            into[pl.ds(low_row, vecs), at] = low[r]

    def collect(n, a, b):
        re = a[:, :nb] * b[:, :nb] - a[:, nb:] * b[:, nb:]
        im = a[:, :nb] * b[:, nb:] + a[:, nb:] * b[:, :nb]
        for i, value in ((n, jnp.sum(re, axis=0)), (6 + n, jnp.sum(im, axis=0))):
            sums[i] = value if sums[i] is None else sums[i] + value

    def own_power(k, z):
        return e2[z, :rows] if k == 2 else (e0, e1)[k][z + 2, lo:hi]

    def take(k, z):
        u = own_power(k, z)
        split(stack, k * vecs, (4 + k) * vecs, z, u)
        if k:
            collect(2 * k - 1, own_power(k - 1, z), u)
        collect(2 * k, u, u)

    def take_last(z):
        u2 = own_power(2, z)
        beside = e2[z + 1, :rows] + e2[z, 1:rows + 1] + roll_y(u2, lanes - 1)
        y = 0.5 * (diag[z + 2, lo:hi] * u2 - beside)
        split(last, 0, vecs, z, y)
        collect(5, u2, y)

    def products(a, b):
        return lax.dot_general(
            a, b, (((1,), (1,)), ((), ())), preferred_element_type=jnp.float32
        )

    def cells_of(z, count):
        return pl.ds(z * rows * lanes, count * rows * lanes)

    def squares(z, count):
        block = stack[:, cells_of(z, count)]
        return products(block, block)

    def last_products(z, count):
        at = cells_of(z, count)
        second = jnp.concatenate(
            [stack[pl.ds(2 * vecs, vecs), at], stack[pl.ds(6 * vecs, vecs), at]], axis=0
        )
        return products(second, last[:, at])

    def fold(full):
        h = full.shape[0] // 2
        return full[:h, :h] + (full[:h, h:] + full[h:, :h] + full[h:, h:])

    for z in range(planes):
        spread(pot_ref, z, z + 2)
    for z in inner:
        first_power(z, 1, rows + 4)
    for z in range(planes):
        take(0, z)
    for z in inner:
        take(1, z)
    for copy in near:
        copy.wait_recv()
    for z in outer:
        first_power(z, 1, rows + 4)
    spread(pot_halo, 0, 1)
    spread(pot_halo, 1, planes + 2)
    spread(pot_halo, 2, planes + 3)
    for z in inner:
        second_power(z)
    for z in outer:
        take(1, z)
    for z in inner:
        take(2, z)
    for z in range(1, planes - 2):
        take_last(z)
    full = squares(1, planes - 2)
    for copy in far:
        copy.wait_recv()
    first_power(-1, 2, rows + 3)
    first_power(planes, 1, rows + 3)
    for z in outer:
        second_power(z)
    stores = [
        pltpu.make_async_copy(src, basis_hbm.at[k], store.at[k])
        for k, src in enumerate((
            e0.at[pl.ds(2, planes), own],
            e1.at[pl.ds(2, planes), own],
            e2.at[pl.ds(0, planes), pl.ds(0, rows)],
        ))
    ]
    for copy in stores:
        copy.start()
    for z in outer:
        take(2, z)
    take_last(0)
    take_last(planes - 2)
    full = full + squares(0, 1) + squares(planes - 1, 1)
    m = last_products(0, planes - 1)
    farthest.wait_recv()
    first_power(planes + 1)
    second_power(planes, 2, rows + 2)
    take_last(planes - 1)
    m = fold(m + last_products(planes - 1, 1))
    s = fold(full)

    lane = lax.broadcasted_iota(jnp.int32, (nb, lanes), 1)
    row = lax.broadcasted_iota(jnp.int32, (nb, lanes), 0)
    to_left = lanes - nb

    def parts(block):
        re, im = block[:nb], block[nb:]
        return re + pltpu.roll(im, to_left, 1), pltpu.roll(re, to_left, 1) - im

    packed = []
    for k in range(3):
        re, im = parts(s[k * vecs:(k + 1) * vecs])
        packed.append(jnp.where(row <= lax.rem(lane, vecs), re, im))
    pieces = [
        packed[0], pltpu.roll(packed[0], to_left, 1),
        packed[1], pltpu.roll(packed[1], to_left, 1), packed[2],
    ]
    m = jnp.concatenate([m, jnp.zeros((vecs, lanes - vecs), jnp.float32)], axis=1)
    re, im = parts(m)
    pieces += [pltpu.roll(re, 5 * nb, 1), pltpu.roll(im, 6 * nb, 1)]
    out = pieces[0]
    for n in range(1, 7):
        out = jnp.where(lane >= n * nb, pieces[n], out)
    for n in range(12):
        value = jnp.sum(sums[n], axis=1, keepdims=True)
        out = jnp.where(lane == 7 * nb + n, value * (2.0 if n in (5, 11) else 1.0), out)
    payload[0] = out

    def exchange(source, landing, axis, count, me, send_sem, recv_sem):
        sent = []
        for d in range(1, count):
            copy = pltpu.make_async_remote_copy(
                src_ref=source, dst_ref=landing.at[me], send_sem=send_sem.at[d],
                recv_sem=recv_sem.at[d], device_id={axis: lax.rem(me + d, count)},
                device_id_type=MESH,
            )
            copy.start()
            sent.append(copy)
        landing[me] = source[...]
        for copy in sent:
            copy.wait_recv()
        total = landing[0]
        for i in range(1, count):
            total = total + landing[i]
        return total, sent

    total, sent = exchange(payload.at[0], from_slab, "slab", slabs, slab, slab_send, slab_recv)
    copies += sent
    payload[1] = total
    total, sent = exchange(payload.at[1], from_pole, "pole", poles, pole, pole_send, pole_recv)
    copies += sent
    packed_ref[...] = total
    for copy in copies:
        copy.wait_send()
    for copy in stores:
        copy.wait()


def filter_kernel(
    cells, poles, basis_hbm, packed_ref, f_hbm, corr_ref, en_ref, basis, f_ref, fetch, store
):
    _, planes, rows, vecs, lanes = basis.shape
    nb = vecs // 2
    bring = pltpu.make_async_copy(basis_hbm, basis, fetch)
    bring.start()
    packed = packed_ref[...]
    lane = lax.broadcasted_iota(jnp.int32, (nb, lanes), 1)
    row = lax.broadcasted_iota(jnp.int32, (nb, lanes), 0)

    def column(n):
        at = 7 * nb + n
        return jnp.broadcast_to(packed[:, at:at + 1], (nb, lanes))

    moments = [(column(n), column(6 + n)) for n in range(6)]
    shift_re = jnp.zeros((nb, lanes), jnp.float32)
    shift_im, weight_re, weight_im = shift_re, shift_re, shift_re
    for j in range(poles):
        theta = 2.0 * math.pi / poles * (j + 0.5)
        c, t = math.cos(theta), math.sin(theta)
        here = lane >= 0 if j == 0 else lane == j
        shift_re = jnp.where(here, CENTER - BASE + RADIUS * c, shift_re)
        shift_im = jnp.where(here, RADIUS * t, shift_im)
        weight_re = jnp.where(lane == j, RADIUS * c / poles, weight_re)
        weight_im = jnp.where(lane == j, RADIUS * t / poles, weight_im)
    coefs = []
    for x in cocg_coefficients(moments, (shift_re, shift_im)):
        x = cmul((weight_re, weight_im), x)
        coefs.append(
            tuple(jnp.broadcast_to(jnp.sum(c, axis=1, keepdims=True), (nb, lanes)) for c in x)
        )

    bring.wait()
    for z in range(planes):
        re = im = None
        for (cr, ci), u in zip(coefs, (basis[0, z], basis[1, z], basis[2, z])):
            ur, ui = u[:, :nb], u[:, nb:]
            tr, ti = cr * ur - ci * ui, cr * ui + ci * ur
            re, im = (tr, ti) if re is None else (re + tr, im + ti)
        for r in range(rows):
            both = jnp.concatenate([re[r], im[r]], axis=0)
            f_ref[pl.ds(z * rows + r, vecs, stride=planes * rows), :] = both

    keep = pltpu.make_async_copy(f_ref, f_hbm, store)
    keep.start()

    square = jnp.concatenate([packed, jnp.zeros((lanes - nb, lanes), jnp.float32)], axis=0)
    turned = jnp.transpose(square)

    def piece(n):
        here = packed if n == 0 else pltpu.roll(packed, lanes - n * nb, 1)
        return here, turned[n * nb:(n + 1) * nb]

    grams = []
    for n in range(5):
        here, across = piece(n)
        re = jnp.where(row <= lane, here, across)
        im = jnp.where(row > lane, here, jnp.where(row < lane, -across, 0.0))
        grams.append((re, im))
    (re, re_t), (im, im_t) = piece(5), piece(6)
    grams.append((re + re_t, im - im_t))
    across = [
        tuple(jnp.sum(jnp.where(lane == row, c, 0.0), axis=0, keepdims=True) for c in coef)
        for coef in coefs
    ]

    def quadratic(first_power):
        out = None
        for l in range(3):
            term = None
            for k in range(3):
                t = cmul_conj(coefs[k], grams[k + l + first_power])
                term = t if term is None else cadd(term, t)
            term = cmul(term, across[l])
            out = term if out is None else cadd(out, term)
        return out

    corr = quadratic(0)
    energy = quadratic(1)
    for i in range(2):
        corr_ref[i] = (corr[i] / cells)[:, :nb]
        en_ref[i] = ((energy[i] + BASE * corr[i]) / cells)[:, :nb]
    keep.wait()


def on_device(slabs, poles, vectors, potential):
    _, nb, planes, nx, ny = vectors.shape
    rows = nx // poles
    vecs = 2 * nb
    cells = float(planes * slabs * nx * ny)
    vmem = pl.BlockSpec(memory_space=pltpu.VMEM)
    whole = pl.BlockSpec(memory_space=pl.ANY)
    dma = pltpu.SemaphoreType.DMA
    scratch = lambda *shape: pltpu.VMEM(shape, jnp.float32)
    limit = 63 * 1024 * 1024
    basis, packed = pl.pallas_call(
        functools.partial(gather_kernel, slabs, poles),
        out_shape=(
            jax.ShapeDtypeStruct((3, planes, rows, vecs, ny), jnp.float32),
            jax.ShapeDtypeStruct((nb, ny), jnp.float32),
        ),
        in_specs=[whole, whole],
        out_specs=(whole, vmem),
        scratch_shapes=[
            scratch(planes, vecs, nx, ny),
            scratch(planes, nx, ny),
            scratch(planes + 5, rows + 5, vecs, ny),
            scratch(planes + 4, rows + 5, vecs, ny),
            scratch(planes + 1, rows + 1, vecs, ny),
            scratch(3, nx, ny),
            scratch(planes + 4, rows + 5, vecs, ny),
            pltpu.VMEM((8 * vecs, planes * rows * ny), jnp.bfloat16),
            pltpu.VMEM((2 * vecs, planes * rows * ny), jnp.bfloat16),
            scratch(2, nb, ny),
            scratch(slabs, nb, ny),
            scratch(poles, nb, ny),
            dma((planes + 1,)),
            dma((3,)),
            dma((7,)),
            dma((7,)),
            dma((slabs,)),
            dma((slabs,)),
            dma((poles,)),
            dma((poles,)),
        ],
        compiler_params=pltpu.CompilerParams(
            collective_id=0, has_side_effects=True, vmem_limit_bytes=limit
        ),
    )(vectors.reshape(vecs, planes, nx, ny), potential)
    filtered, corr, energy = pl.pallas_call(
        functools.partial(filter_kernel, cells, poles),
        out_shape=(
            jax.ShapeDtypeStruct((vecs * planes * rows, ny), jnp.float32),
            jax.ShapeDtypeStruct((2, nb, nb), jnp.float32),
            jax.ShapeDtypeStruct((2, nb, nb), jnp.float32),
        ),
        in_specs=[whole, vmem],
        out_specs=(whole, vmem, vmem),
        scratch_shapes=[
            scratch(3, planes, rows, vecs, ny), scratch(vecs * planes * rows, ny), dma, dma
        ],
        compiler_params=pltpu.CompilerParams(vmem_limit_bytes=limit),
    )(basis, packed)
    return filtered.reshape(2, nb, planes, rows, ny), corr, energy


def solution(mesh):
    in_specs = (P(None, None, "slab", None, None), P("slab", None, None))
    out_specs = (P(None, None, "slab", "pole", None), P(), P())
    body = functools.partial(on_device, mesh.shape["slab"], mesh.shape["pole"])
    return jax.shard_map(
        body, mesh=mesh, in_specs=in_specs, out_specs=out_specs, check_vma=False
    )
```

```python
import functools
import math

import jax
import jax.numpy as jnp
from jax import lax
from jax.experimental import pallas as pl
from jax.experimental.pallas import tpu as pltpu
from jax.sharding import PartitionSpec as P

ITERS = 3
CENTER = 2.0
RADIUS = 1.5
BASE = 4.0

MESH = pl.DeviceIdType.MESH


def cmul(a, b):
    return (a[0] * b[0] - a[1] * b[1], a[0] * b[1] + a[1] * b[0])


def cmul_conj(a, b):
    return (a[0] * b[0] + a[1] * b[1], a[0] * b[1] - a[1] * b[0])


def cadd(a, b):
    return (a[0] + b[0], a[1] + b[1])


def csub(a, b):
    return (a[0] - b[0], a[1] - b[1])


def cdiv(n, d):
    inv = 1.0 / (d[0] * d[0] + d[1] * d[1])
    return ((n[0] * d[0] + n[1] * d[1]) * inv, (n[1] * d[0] - n[0] * d[1]) * inv)


def cocg_coefficients(moments, shift):
    def form(a, b):
        anti = {}
        for i, ai in enumerate(a):
            for j, bj in enumerate(b):
                term = bj if ai is None else cmul(ai, bj)
                anti[i + j] = cadd(anti[i + j], term) if i + j in anti else term
        total = None
        for n, coef in anti.items():
            term = cmul(coef, moments[n])
            total = term if total is None else cadd(total, term)
        return total

    one = (jnp.ones_like(shift[0]), jnp.zeros_like(shift[0]))
    x = []
    r = [one]
    p = [one]
    rho = moments[0]
    for iteration in range(ITERS):
        q = [cmul(shift, c) for c in p] + [None]
        for i, c in enumerate(p):
            q[i + 1] = (-c[0], -c[1]) if q[i + 1] is None else csub(q[i + 1], c)
        alpha = cdiv(rho, form(p, q))
        step = [cmul(alpha, c) for c in p]
        x = [cadd(x[i], c) if i < len(x) else c for i, c in enumerate(step)]
        if iteration + 1 < ITERS:
            down = [cmul(alpha, c) for c in q]
            r = [csub(r[i], c) if i < len(r) else (-c[0], -c[1]) for i, c in enumerate(down)]
            rho_new = form(r, r)
            beta = cdiv(rho_new, rho)
            p = [cadd(c, cmul(beta, p[i])) if i < len(p) else c for i, c in enumerate(r)]
            rho = rho_new
    return x


def gather_kernel(
    slabs, poles, v_hbm, pot_hbm, basis_hbm, packed_ref,
    v_ref, pot_ref, e0, e1, e2, pot_halo, diag, stack, last, payload, from_slab, from_pole,
    fetch, store, halo_send, halo_recv, slab_send, slab_recv, pole_send, pole_recv,
):
    planes, nx, lanes = pot_ref.shape
    vecs = e0.shape[2]
    nb = vecs // 2
    rows = basis_hbm.shape[2]
    slab = lax.axis_index("slab")
    pole = lax.axis_index("pole")
    x0 = pole * rows
    ahead = lax.rem(pole + 1, poles)
    back = lax.rem(pole + poles - 1, poles)
    up = lax.rem(slab + 1, slabs)
    down = lax.rem(slab + slabs - 1, slabs)

    order = [0, planes - 1] + list(range(1, planes - 1))
    fetches = {
        z: pltpu.make_async_copy(v_hbm.at[:, z], v_ref.at[z], fetch.at[z]) for z in order
    }
    fetch_pot = pltpu.make_async_copy(pot_hbm, pot_ref, fetch.at[planes])
    for z in order:
        fetches[z].start()
    fetch_pot.start()

    barrier = pltpu.get_barrier_semaphore()
    for d in range(1, slabs):
        pl.semaphore_signal(
            barrier, inc=1, device_id={"slab": lax.rem(slab + d, slabs)}, device_id_type=MESH
        )
    for d in range(1, poles):
        pl.semaphore_signal(
            barrier, inc=1, device_id={"pole": lax.rem(pole + d, poles)}, device_id_type=MESH
        )
    empty = jnp.zeros((vecs, stack.shape[1]), stack.dtype)
    stack[pl.ds(3 * vecs, vecs)] = empty
    stack[pl.ds(7 * vecs, vecs)] = empty

    def window(q):
        return lax.rem(x0 + (q - 2 + nx), nx)

    lines = v_ref.reshape(planes * vecs * nx, lanes)

    def gather(z):
        fetches[z].wait()
        for q in range(rows + 4):
            e0[z + 2, q] = lines[pl.ds(z * vecs * nx + window(q), vecs, stride=nx), :]

    copies = []

    def send(i, src, dst, axis, target):
        copy = pltpu.make_async_remote_copy(
            src_ref=src, dst_ref=dst, send_sem=halo_send.at[i], recv_sem=halo_recv.at[i],
            device_id={axis: target}, device_id_type=MESH,
        )
        copy.start()
        copies.append(copy)
        return copy

    own = pl.ds(2, rows)

    def send_plane(i, z, there, target):
        return send(i, e0.at[z + 2, own], e0.at[there + 2, own], "slab", target)

    gather(0)
    gather(planes - 1)
    fetch_pot.wait()
    pl.semaphore_wait(barrier, slabs - 1 + poles - 1)
    near = [
        send_plane(2, planes - 1, -1, up),
        send_plane(3, 0, planes, down),
        send(0, pot_ref.at[planes - 1], pot_halo.at[0], "slab", up),
        send(1, pot_ref.at[0], pot_halo.at[1], "slab", down),
    ]
    for z in range(1, planes - 1):
        gather(z)
    far = [
        send_plane(4, planes - 2, -2, up),
        send_plane(5, 1, planes + 1, down),
    ]

    def spread(ref, z, p):
        for q in range(1, rows + 3):
            line = ref[z, pl.ds(window(q), 1), :] + (3.0 - BASE)
            diag[p, q] = jnp.broadcast_to(line, (vecs, lanes))

    def roll_y(block, by):
        flat = block.reshape(block.shape[0] * vecs, lanes)
        return pltpu.roll(flat, by, 1).reshape(block.shape)

    def apply(src, z, lo, hi):
        p = z + 2
        here = src[p, lo:hi]
        beside = src[p - 1, lo:hi] + src[p + 1, lo:hi]
        beside = beside + src[p, lo - 1:hi - 1] + src[p, lo + 1:hi + 1]
        beside = beside + (roll_y(here, 1) + roll_y(here, lanes - 1))
        return diag[p, lo:hi] * here - 0.5 * beside

    def first_power(z, lo=2, hi=rows + 2):
        e1[z + 2, lo:hi] = apply(e0, z, lo, hi)

    def second_power(z):
        e2[z, :rows] = apply(e1, z, 2, rows + 2)

    def pass_row(i, z, count):
        at = pl.ds(z, count)
        return send(i, e2.at[at, 0], e2.at[at, rows], "pole", back)

    lo, hi = 2, rows + 2
    sums = [None] * 12
    inner, outer = range(1, planes - 1), (0, planes - 1)

    def split(into, high_row, low_row, z, u):
        high = u.astype(jnp.bfloat16)
        low = (u - high.astype(jnp.float32)).astype(jnp.bfloat16)
        for r in range(rows):
            at = pl.ds((z * rows + r) * lanes, lanes)
            into[pl.ds(high_row, vecs), at] = high[r]
            into[pl.ds(low_row, vecs), at] = low[r]

    def collect(n, a, b):
        re = a[:, :nb] * b[:, :nb] - a[:, nb:] * b[:, nb:]
        im = a[:, :nb] * b[:, nb:] + a[:, nb:] * b[:, :nb]
        for i, value in ((n, jnp.sum(re, axis=0)), (6 + n, jnp.sum(im, axis=0))):
            sums[i] = value if sums[i] is None else sums[i] + value

    def own_power(k, z):
        return e2[z, :rows] if k == 2 else (e0, e1)[k][z + 2, lo:hi]

    def take(k, z):
        u = own_power(k, z)
        split(stack, k * vecs, (4 + k) * vecs, z, u)
        if k:
            collect(2 * k - 1, own_power(k - 1, z), u)
        collect(2 * k, u, u)

    def take_last(z):
        u2 = own_power(2, z)
        beside = e2[z + 1, :rows] + e2[z, 1:rows + 1] + roll_y(u2, lanes - 1)
        y = 0.5 * (diag[z + 2, lo:hi] * u2 - beside)
        split(last, 0, vecs, z, y)
        collect(5, u2, y)

    def products(a, b):
        return lax.dot_general(
            a, b, (((1,), (1,)), ((), ())), preferred_element_type=jnp.float32
        )

    def cells_of(z, count):
        return pl.ds(z * rows * lanes, count * rows * lanes)

    def squares(z, count):
        block = stack[:, cells_of(z, count)]
        return products(block, block)

    def last_products(z, count):
        at = cells_of(z, count)
        second = jnp.concatenate(
            [stack[pl.ds(2 * vecs, vecs), at], stack[pl.ds(6 * vecs, vecs), at]], axis=0
        )
        return products(second, last[:, at])

    def fold(full):
        h = full.shape[0] // 2
        return full[:h, :h] + (full[:h, h:] + full[h:, :h] + full[h:, h:])

    for z in range(planes):
        spread(pot_ref, z, z + 2)
    for z in inner:
        first_power(z, 1, rows + 3)
    for z in range(planes):
        take(0, z)
    for z in inner:
        take(1, z)
    for copy in near:
        copy.wait_recv()
    sides = []
    for i, p in ((6, 1), (8, planes + 2)):
        sides.append(send(i, e0.at[p, 2], e0.at[p, rows + 2], "pole", back))
        sides.append(send(i + 1, e0.at[p, rows + 1], e0.at[p, 1], "pole", ahead))
    for z in outer:
        first_power(z)
    spread(pot_halo, 0, 1)
    spread(pot_halo, 1, planes + 2)
    for z in inner:
        second_power(z)
    beside_inner = pass_row(10, 1, planes - 2)
    for z in outer:
        take(1, z)
    for z in inner:
        take(2, z)
    for copy in sides:
        copy.wait_recv()
    for z in outer:
        first_power(z, 1, 2)
        first_power(z, rows + 2, rows + 3)
    for copy in far:
        copy.wait_recv()
    first_power(-1)
    second_power(0)
    edge = send(11, e2.at[0, pl.ds(0, rows)], e2.at[planes, pl.ds(0, rows)], "slab", down)
    first_power(planes)
    second_power(planes - 1)
    beside_outer = [pass_row(12, 0, 1), pass_row(13, planes - 1, 1)]
    stores = [
        pltpu.make_async_copy(src, basis_hbm.at[k], store.at[k])
        for k, src in enumerate((
            e0.at[pl.ds(2, planes), own],
            e1.at[pl.ds(2, planes), own],
            e2.at[pl.ds(0, planes), pl.ds(0, rows)],
        ))
    ]
    for copy in stores:
        copy.start()
    for z in outer:
        take(2, z)
    full = squares(0, planes)
    beside_inner.wait_recv()
    for z in inner:
        take_last(z)
    for copy in beside_outer:
        copy.wait_recv()
    take_last(0)
    m = last_products(0, planes - 1)
    edge.wait_recv()
    take_last(planes - 1)
    m = fold(m + last_products(planes - 1, 1))
    s = fold(full)

    lane = lax.broadcasted_iota(jnp.int32, (nb, lanes), 1)
    row = lax.broadcasted_iota(jnp.int32, (nb, lanes), 0)
    to_left = lanes - nb

    def parts(block):
        re, im = block[:nb], block[nb:]
        return re + pltpu.roll(im, to_left, 1), pltpu.roll(re, to_left, 1) - im

    packed = []
    for k in range(3):
        re, im = parts(s[k * vecs:(k + 1) * vecs])
        packed.append(jnp.where(row <= lax.rem(lane, vecs), re, im))
    pieces = [
        packed[0], pltpu.roll(packed[0], to_left, 1),
        packed[1], pltpu.roll(packed[1], to_left, 1), packed[2],
    ]
    m = jnp.concatenate([m, jnp.zeros((vecs, lanes - vecs), jnp.float32)], axis=1)
    re, im = parts(m)
    pieces += [pltpu.roll(re, 5 * nb, 1), pltpu.roll(im, 6 * nb, 1)]
    out = pieces[0]
    for n in range(1, 7):
        out = jnp.where(lane >= n * nb, pieces[n], out)
    for n in range(12):
        value = jnp.sum(sums[n], axis=1, keepdims=True)
        out = jnp.where(lane == 7 * nb + n, value * (2.0 if n in (5, 11) else 1.0), out)
    payload[0] = out

    def exchange(source, landing, axis, count, me, send_sem, recv_sem):
        sent = []
        for d in range(1, count):
            copy = pltpu.make_async_remote_copy(
                src_ref=source, dst_ref=landing.at[me], send_sem=send_sem.at[d],
                recv_sem=recv_sem.at[d], device_id={axis: lax.rem(me + d, count)},
                device_id_type=MESH,
            )
            copy.start()
            sent.append(copy)
        landing[me] = source[...]
        for copy in sent:
            copy.wait_recv()
        total = landing[0]
        for i in range(1, count):
            total = total + landing[i]
        return total, sent

    total, sent = exchange(payload.at[0], from_slab, "slab", slabs, slab, slab_send, slab_recv)
    copies += sent
    payload[1] = total
    total, sent = exchange(payload.at[1], from_pole, "pole", poles, pole, pole_send, pole_recv)
    copies += sent
    packed_ref[...] = total
    for copy in copies:
        copy.wait_send()
    for copy in stores:
        copy.wait()


def filter_kernel(cells, poles, basis_hbm, packed_ref, f_ref, corr_ref, en_ref, basis, fetch):
    _, planes, rows, vecs, lanes = basis.shape
    nb = vecs // 2
    bring = pltpu.make_async_copy(basis_hbm, basis, fetch)
    bring.start()
    packed = packed_ref[...]
    lane = lax.broadcasted_iota(jnp.int32, (nb, lanes), 1)
    row = lax.broadcasted_iota(jnp.int32, (nb, lanes), 0)

    def column(n):
        at = 7 * nb + n
        return jnp.broadcast_to(packed[:, at:at + 1], (nb, lanes))

    moments = [(column(n), column(6 + n)) for n in range(6)]
    shift_re = jnp.zeros((nb, lanes), jnp.float32)
    shift_im, weight_re, weight_im = shift_re, shift_re, shift_re
    for j in range(poles):
        theta = 2.0 * math.pi / poles * (j + 0.5)
        c, t = math.cos(theta), math.sin(theta)
        here = lane >= 0 if j == 0 else lane == j
        shift_re = jnp.where(here, CENTER - BASE + RADIUS * c, shift_re)
        shift_im = jnp.where(here, RADIUS * t, shift_im)
        weight_re = jnp.where(lane == j, RADIUS * c / poles, weight_re)
        weight_im = jnp.where(lane == j, RADIUS * t / poles, weight_im)
    coefs = []
    for x in cocg_coefficients(moments, (shift_re, shift_im)):
        x = cmul((weight_re, weight_im), x)
        coefs.append(
            tuple(jnp.broadcast_to(jnp.sum(c, axis=1, keepdims=True), (nb, lanes)) for c in x)
        )

    bring.wait()
    for z in range(planes):
        re = im = None
        for (cr, ci), u in zip(coefs, (basis[0, z], basis[1, z], basis[2, z])):
            ur, ui = u[:, :nb], u[:, nb:]
            tr, ti = cr * ur - ci * ui, cr * ui + ci * ur
            re, im = (tr, ti) if re is None else (re + tr, im + ti)
        for r in range(rows):
            both = jnp.concatenate([re[r], im[r]], axis=0)
            f_ref[pl.ds(z * rows + r, vecs, stride=planes * rows), :] = both

    square = jnp.concatenate([packed, jnp.zeros((lanes - nb, lanes), jnp.float32)], axis=0)
    turned = jnp.transpose(square)

    def piece(n):
        here = packed if n == 0 else pltpu.roll(packed, lanes - n * nb, 1)
        return here, turned[n * nb:(n + 1) * nb]

    grams = []
    for n in range(5):
        here, across = piece(n)
        re = jnp.where(row <= lane, here, across)
        im = jnp.where(row > lane, here, jnp.where(row < lane, -across, 0.0))
        grams.append((re, im))
    (re, re_t), (im, im_t) = piece(5), piece(6)
    grams.append((re + re_t, im - im_t))
    across = [
        tuple(jnp.sum(jnp.where(lane == row, c, 0.0), axis=0, keepdims=True) for c in coef)
        for coef in coefs
    ]

    def quadratic(first_power):
        out = None
        for l in range(3):
            term = None
            for k in range(3):
                t = cmul_conj(coefs[k], grams[k + l + first_power])
                term = t if term is None else cadd(term, t)
            term = cmul(term, across[l])
            out = term if out is None else cadd(out, term)
        return out

    corr = quadratic(0)
    energy = quadratic(1)
    for i in range(2):
        corr_ref[i] = (corr[i] / cells)[:, :nb]
        en_ref[i] = ((energy[i] + BASE * corr[i]) / cells)[:, :nb]


def on_device(slabs, poles, vectors, potential):
    _, nb, planes, nx, ny = vectors.shape
    rows = nx // poles
    vecs = 2 * nb
    cells = float(planes * slabs * nx * ny)
    vmem = pl.BlockSpec(memory_space=pltpu.VMEM)
    whole = pl.BlockSpec(memory_space=pl.ANY)
    dma = pltpu.SemaphoreType.DMA
    scratch = lambda *shape: pltpu.VMEM(shape, jnp.float32)
    limit = 63 * 1024 * 1024
    basis, packed = pl.pallas_call(
        functools.partial(gather_kernel, slabs, poles),
        out_shape=(
            jax.ShapeDtypeStruct((3, planes, rows, vecs, ny), jnp.float32),
            jax.ShapeDtypeStruct((nb, ny), jnp.float32),
        ),
        in_specs=[whole, whole],
        out_specs=(whole, vmem),
        scratch_shapes=[
            scratch(planes, vecs, nx, ny),
            scratch(planes, nx, ny),
            scratch(planes + 4, rows + 4, vecs, ny),
            scratch(planes + 4, rows + 4, vecs, ny),
            scratch(planes + 1, rows + 1, vecs, ny),
            scratch(2, nx, ny),
            scratch(planes + 4, rows + 4, vecs, ny),
            pltpu.VMEM((8 * vecs, planes * rows * ny), jnp.bfloat16),
            pltpu.VMEM((2 * vecs, planes * rows * ny), jnp.bfloat16),
            scratch(2, nb, ny),
            scratch(slabs, nb, ny),
            scratch(poles, nb, ny),
            dma((planes + 1,)),
            dma((3,)),
            dma((14,)),
            dma((14,)),
            dma((slabs,)),
            dma((slabs,)),
            dma((poles,)),
            dma((poles,)),
        ],
        compiler_params=pltpu.CompilerParams(
            collective_id=0, has_side_effects=True, vmem_limit_bytes=limit
        ),
    )(vectors.reshape(vecs, planes, nx, ny), potential)
    filtered, corr, energy = pl.pallas_call(
        functools.partial(filter_kernel, cells, poles),
        out_shape=(
            jax.ShapeDtypeStruct((vecs * planes * rows, ny), jnp.float32),
            jax.ShapeDtypeStruct((2, nb, nb), jnp.float32),
            jax.ShapeDtypeStruct((2, nb, nb), jnp.float32),
        ),
        in_specs=[whole, vmem],
        out_specs=(vmem, vmem, vmem),
        scratch_shapes=[scratch(3, planes, rows, vecs, ny), dma],
        compiler_params=pltpu.CompilerParams(vmem_limit_bytes=limit),
    )(basis, packed)
    return filtered.reshape(2, nb, planes, rows, ny), corr, energy


def solution(mesh):
    in_specs = (P(None, None, "slab", None, None), P("slab", None, None))
    out_specs = (P(None, None, "slab", "pole", None), P(), P())
    body = functools.partial(on_device, mesh.shape["slab"], mesh.shape["pole"])
    return jax.shard_map(
        body, mesh=mesh, in_specs=in_specs, out_specs=out_specs, check_vma=False
    )
```

```python
import functools
import math

import jax
import jax.numpy as jnp
from jax import lax
from jax.experimental import pallas as pl
from jax.experimental.pallas import tpu as pltpu
from jax.sharding import PartitionSpec as P

ITERS = 3
CENTER = 2.0
RADIUS = 1.5
BASE = 4.0

MESH = pl.DeviceIdType.MESH


def cmul(a, b):
    return (a[0] * b[0] - a[1] * b[1], a[0] * b[1] + a[1] * b[0])


def cmul_conj(a, b):
    return (a[0] * b[0] + a[1] * b[1], a[0] * b[1] - a[1] * b[0])


def cadd(a, b):
    return (a[0] + b[0], a[1] + b[1])


def csub(a, b):
    return (a[0] - b[0], a[1] - b[1])


def cdiv(n, d):
    inv = 1.0 / (d[0] * d[0] + d[1] * d[1])
    return ((n[0] * d[0] + n[1] * d[1]) * inv, (n[1] * d[0] - n[0] * d[1]) * inv)


def cocg_coefficients(moments, shift):
    def form(a, b):
        anti = {}
        for i, ai in enumerate(a):
            for j, bj in enumerate(b):
                term = bj if ai is None else cmul(ai, bj)
                anti[i + j] = cadd(anti[i + j], term) if i + j in anti else term
        total = None
        for n, coef in anti.items():
            term = cmul(coef, moments[n])
            total = term if total is None else cadd(total, term)
        return total

    one = (jnp.ones_like(shift[0]), jnp.zeros_like(shift[0]))
    x = []
    r = [one]
    p = [one]
    rho = moments[0]
    for iteration in range(ITERS):
        q = [cmul(shift, c) for c in p] + [None]
        for i, c in enumerate(p):
            q[i + 1] = (-c[0], -c[1]) if q[i + 1] is None else csub(q[i + 1], c)
        alpha = cdiv(rho, form(p, q))
        step = [cmul(alpha, c) for c in p]
        x = [cadd(x[i], c) if i < len(x) else c for i, c in enumerate(step)]
        if iteration + 1 < ITERS:
            down = [cmul(alpha, c) for c in q]
            r = [csub(r[i], c) if i < len(r) else (-c[0], -c[1]) for i, c in enumerate(down)]
            rho_new = form(r, r)
            beta = cdiv(rho_new, rho)
            p = [cadd(c, cmul(beta, p[i])) if i < len(p) else c for i, c in enumerate(r)]
            rho = rho_new
    return x


def gather_kernel(
    slabs, poles, v_hbm, pot_hbm, basis_hbm, packed_ref,
    v_ref, pot_ref, e0, e1, e2, pot_halo, diag, stack, last, payload, from_slab, from_pole,
    fetch, store, halo_send, halo_recv, slab_send, slab_recv, pole_send, pole_recv,
):
    planes, nx, lanes = pot_ref.shape
    vecs = e0.shape[2]
    nb = vecs // 2
    rows = basis_hbm.shape[2]
    slab = lax.axis_index("slab")
    pole = lax.axis_index("pole")
    x0 = pole * rows
    ahead = lax.rem(pole + 1, poles)
    back = lax.rem(pole + poles - 1, poles)
    up = lax.rem(slab + 1, slabs)
    down = lax.rem(slab + slabs - 1, slabs)

    order = [0, planes - 1] + list(range(1, planes - 1))
    fetches = {
        z: pltpu.make_async_copy(v_hbm.at[:, z], v_ref.at[z], fetch.at[z]) for z in order
    }
    fetch_pot = pltpu.make_async_copy(pot_hbm, pot_ref, fetch.at[planes])
    for z in order:
        fetches[z].start()
    fetch_pot.start()

    barrier = pltpu.get_barrier_semaphore()
    for d in range(1, slabs):
        pl.semaphore_signal(
            barrier, inc=1, device_id={"slab": lax.rem(slab + d, slabs)}, device_id_type=MESH
        )
    for d in range(1, poles):
        pl.semaphore_signal(
            barrier, inc=1, device_id={"pole": lax.rem(pole + d, poles)}, device_id_type=MESH
        )
    empty = jnp.zeros((vecs, stack.shape[1]), stack.dtype)
    stack[pl.ds(3 * vecs, vecs)] = empty
    stack[pl.ds(7 * vecs, vecs)] = empty

    def window(q):
        return lax.rem(x0 + (q - 2 + nx), nx)

    lines = v_ref.reshape(planes * vecs * nx, lanes)

    def gather(z):
        fetches[z].wait()
        for q in range(rows + 4):
            e0[z + 2, q] = lines[pl.ds(z * vecs * nx + window(q), vecs, stride=nx), :]

    copies = []

    def send(i, src, dst, axis, target):
        copy = pltpu.make_async_remote_copy(
            src_ref=src, dst_ref=dst, send_sem=halo_send.at[i], recv_sem=halo_recv.at[i],
            device_id={axis: target}, device_id_type=MESH,
        )
        copy.start()
        copies.append(copy)
        return copy

    own = pl.ds(2, rows)

    def send_plane(i, z, there, target):
        return send(i, e0.at[z + 2, own], e0.at[there + 2, own], "slab", target)

    gather(0)
    gather(planes - 1)
    fetch_pot.wait()
    pl.semaphore_wait(barrier, slabs - 1 + poles - 1)
    near = [
        send_plane(2, planes - 1, -1, up),
        send_plane(3, 0, planes, down),
        send(0, pot_ref.at[planes - 1], pot_halo.at[0], "slab", up),
        send(1, pot_ref.at[pl.ds(0, 2)], pot_halo.at[pl.ds(1, 2)], "slab", down),
    ]
    for z in range(1, planes - 1):
        gather(z)
    far = [
        send_plane(4, planes - 2, -2, up),
        send_plane(5, 1, planes + 1, down),
    ]
    farthest = send_plane(11, 2, planes + 2, down)

    def spread(ref, z, p):
        for q in range(1, rows + 3):
            line = ref[z, pl.ds(window(q), 1), :] + (3.0 - BASE)
            diag[p, q] = jnp.broadcast_to(line, (vecs, lanes))

    def roll_y(block, by):
        flat = block.reshape(block.shape[0] * vecs, lanes)
        return pltpu.roll(flat, by, 1).reshape(block.shape)

    def apply(src, z, lo, hi):
        p = z + 2
        here = src[p, lo:hi]
        beside = src[p - 1, lo:hi] + src[p + 1, lo:hi]
        beside = beside + src[p, lo - 1:hi - 1] + src[p, lo + 1:hi + 1]
        beside = beside + (roll_y(here, 1) + roll_y(here, lanes - 1))
        return diag[p, lo:hi] * here - 0.5 * beside

    def first_power(z, lo=2, hi=rows + 2):
        e1[z + 2, lo:hi] = apply(e0, z, lo, hi)

    def second_power(z):
        e2[z, :rows] = apply(e1, z, 2, rows + 2)

    def pass_row(i, z, count):
        at = pl.ds(z, count)
        return send(i, e2.at[at, 0], e2.at[at, rows], "pole", back)

    lo, hi = 2, rows + 2
    sums = [None] * 12
    inner, outer = range(1, planes - 1), (0, planes - 1)

    def split(into, high_row, low_row, z, u):
        high = u.astype(jnp.bfloat16)
        low = (u - high.astype(jnp.float32)).astype(jnp.bfloat16)
        for r in range(rows):
            at = pl.ds((z * rows + r) * lanes, lanes)
            into[pl.ds(high_row, vecs), at] = high[r]
            into[pl.ds(low_row, vecs), at] = low[r]

    def collect(n, a, b):
        re = a[:, :nb] * b[:, :nb] - a[:, nb:] * b[:, nb:]
        im = a[:, :nb] * b[:, nb:] + a[:, nb:] * b[:, :nb]
        for i, value in ((n, jnp.sum(re, axis=0)), (6 + n, jnp.sum(im, axis=0))):
            sums[i] = value if sums[i] is None else sums[i] + value

    def own_power(k, z):
        return e2[z, :rows] if k == 2 else (e0, e1)[k][z + 2, lo:hi]

    def take(k, z):
        u = own_power(k, z)
        split(stack, k * vecs, (4 + k) * vecs, z, u)
        if k:
            collect(2 * k - 1, own_power(k - 1, z), u)
        collect(2 * k, u, u)

    def take_last(z):
        u2 = own_power(2, z)
        beside = e2[z + 1, :rows] + e2[z, 1:rows + 1] + roll_y(u2, lanes - 1)
        y = 0.5 * (diag[z + 2, lo:hi] * u2 - beside)
        split(last, 0, vecs, z, y)
        collect(5, u2, y)

    def products(a, b):
        return lax.dot_general(
            a, b, (((1,), (1,)), ((), ())), preferred_element_type=jnp.float32
        )

    def cells_of(z, count):
        return pl.ds(z * rows * lanes, count * rows * lanes)

    def squares(z, count):
        block = stack[:, cells_of(z, count)]
        return products(block, block)

    def last_products(z, count):
        at = cells_of(z, count)
        second = jnp.concatenate(
            [stack[pl.ds(2 * vecs, vecs), at], stack[pl.ds(6 * vecs, vecs), at]], axis=0
        )
        return products(second, last[:, at])

    def fold(full):
        h = full.shape[0] // 2
        return full[:h, :h] + (full[:h, h:] + full[h:, :h] + full[h:, h:])

    for z in range(planes):
        spread(pot_ref, z, z + 2)
    for z in inner:
        first_power(z, 1, rows + 3)
    for z in range(planes):
        take(0, z)
    for z in inner:
        take(1, z)
    for copy in near:
        copy.wait_recv()

    def pass_sides(i, ref, p):
        return [
            send(i, ref.at[p, 2], ref.at[p, rows + 2], "pole", back),
            send(i + 1, ref.at[p, rows + 1], ref.at[p, 1], "pole", ahead),
        ]

    sides = pass_sides(6, e0, 1) + pass_sides(8, e0, planes + 2)
    for z in outer:
        first_power(z)
    spread(pot_halo, 0, 1)
    spread(pot_halo, 1, planes + 2)
    spread(pot_halo, 2, planes + 3)
    for z in inner:
        second_power(z)
    beside_inner = pass_row(10, 1, planes - 2)
    for z in outer:
        take(1, z)
    for z in inner:
        take(2, z)
    for copy in sides:
        copy.wait_recv()
    for z in outer:
        first_power(z, 1, 2)
        first_power(z, rows + 2, rows + 3)
    for copy in far:
        copy.wait_recv()
    later = pass_sides(14, e0, planes + 3)
    first_power(planes)
    later += pass_sides(16, e1, planes + 2)
    first_power(-1)
    second_power(0)
    second_power(planes - 1)
    beside_outer = [pass_row(12, 0, 1), pass_row(13, planes - 1, 1)]
    stores = [
        pltpu.make_async_copy(src, basis_hbm.at[k], store.at[k])
        for k, src in enumerate((
            e0.at[pl.ds(2, planes), own],
            e1.at[pl.ds(2, planes), own],
            e2.at[pl.ds(0, planes), pl.ds(0, rows)],
        ))
    ]
    for copy in stores:
        copy.start()
    for z in outer:
        take(2, z)
    full = squares(0, planes)
    beside_inner.wait_recv()
    for z in inner:
        take_last(z)
    for copy in beside_outer:
        copy.wait_recv()
    take_last(0)
    m = last_products(0, planes - 1)
    for copy in later:
        copy.wait_recv()
    farthest.wait_recv()
    first_power(planes + 1)
    second_power(planes)
    take_last(planes - 1)
    m = fold(m + last_products(planes - 1, 1))
    s = fold(full)

    lane = lax.broadcasted_iota(jnp.int32, (nb, lanes), 1)
    row = lax.broadcasted_iota(jnp.int32, (nb, lanes), 0)
    to_left = lanes - nb

    def parts(block):
        re, im = block[:nb], block[nb:]
        return re + pltpu.roll(im, to_left, 1), pltpu.roll(re, to_left, 1) - im

    packed = []
    for k in range(3):
        re, im = parts(s[k * vecs:(k + 1) * vecs])
        packed.append(jnp.where(row <= lax.rem(lane, vecs), re, im))
    pieces = [
        packed[0], pltpu.roll(packed[0], to_left, 1),
        packed[1], pltpu.roll(packed[1], to_left, 1), packed[2],
    ]
    m = jnp.concatenate([m, jnp.zeros((vecs, lanes - vecs), jnp.float32)], axis=1)
    re, im = parts(m)
    pieces += [pltpu.roll(re, 5 * nb, 1), pltpu.roll(im, 6 * nb, 1)]
    out = pieces[0]
    for n in range(1, 7):
        out = jnp.where(lane >= n * nb, pieces[n], out)
    for n in range(12):
        value = jnp.sum(sums[n], axis=1, keepdims=True)
        out = jnp.where(lane == 7 * nb + n, value * (2.0 if n in (5, 11) else 1.0), out)
    payload[0] = out

    def exchange(source, landing, axis, count, me, send_sem, recv_sem):
        sent = []
        for d in range(1, count):
            copy = pltpu.make_async_remote_copy(
                src_ref=source, dst_ref=landing.at[me], send_sem=send_sem.at[d],
                recv_sem=recv_sem.at[d], device_id={axis: lax.rem(me + d, count)},
                device_id_type=MESH,
            )
            copy.start()
            sent.append(copy)
        landing[me] = source[...]
        for copy in sent:
            copy.wait_recv()
        total = landing[0]
        for i in range(1, count):
            total = total + landing[i]
        return total, sent

    total, sent = exchange(payload.at[0], from_slab, "slab", slabs, slab, slab_send, slab_recv)
    copies += sent
    payload[1] = total
    total, sent = exchange(payload.at[1], from_pole, "pole", poles, pole, pole_send, pole_recv)
    copies += sent
    packed_ref[...] = total
    for copy in copies:
        copy.wait_send()
    for copy in stores:
        copy.wait()


def filter_kernel(cells, poles, basis_hbm, packed_ref, f_ref, corr_ref, en_ref, basis, fetch):
    _, planes, rows, vecs, lanes = basis.shape
    nb = vecs // 2
    bring = pltpu.make_async_copy(basis_hbm, basis, fetch)
    bring.start()
    packed = packed_ref[...]
    lane = lax.broadcasted_iota(jnp.int32, (nb, lanes), 1)
    row = lax.broadcasted_iota(jnp.int32, (nb, lanes), 0)

    def column(n):
        at = 7 * nb + n
        return jnp.broadcast_to(packed[:, at:at + 1], (nb, lanes))

    moments = [(column(n), column(6 + n)) for n in range(6)]
    shift_re = jnp.zeros((nb, lanes), jnp.float32)
    shift_im, weight_re, weight_im = shift_re, shift_re, shift_re
    for j in range(poles):
        theta = 2.0 * math.pi / poles * (j + 0.5)
        c, t = math.cos(theta), math.sin(theta)
        here = lane >= 0 if j == 0 else lane == j
        shift_re = jnp.where(here, CENTER - BASE + RADIUS * c, shift_re)
        shift_im = jnp.where(here, RADIUS * t, shift_im)
        weight_re = jnp.where(lane == j, RADIUS * c / poles, weight_re)
        weight_im = jnp.where(lane == j, RADIUS * t / poles, weight_im)
    coefs = []
    for x in cocg_coefficients(moments, (shift_re, shift_im)):
        x = cmul((weight_re, weight_im), x)
        coefs.append(
            tuple(jnp.broadcast_to(jnp.sum(c, axis=1, keepdims=True), (nb, lanes)) for c in x)
        )

    bring.wait()
    for z in range(planes):
        re = im = None
        for (cr, ci), u in zip(coefs, (basis[0, z], basis[1, z], basis[2, z])):
            ur, ui = u[:, :nb], u[:, nb:]
            tr, ti = cr * ur - ci * ui, cr * ui + ci * ur
            re, im = (tr, ti) if re is None else (re + tr, im + ti)
        for r in range(rows):
            both = jnp.concatenate([re[r], im[r]], axis=0)
            f_ref[pl.ds(z * rows + r, vecs, stride=planes * rows), :] = both

    square = jnp.concatenate([packed, jnp.zeros((lanes - nb, lanes), jnp.float32)], axis=0)
    turned = jnp.transpose(square)

    def piece(n):
        here = packed if n == 0 else pltpu.roll(packed, lanes - n * nb, 1)
        return here, turned[n * nb:(n + 1) * nb]

    grams = []
    for n in range(5):
        here, across = piece(n)
        re = jnp.where(row <= lane, here, across)
        im = jnp.where(row > lane, here, jnp.where(row < lane, -across, 0.0))
        grams.append((re, im))
    (re, re_t), (im, im_t) = piece(5), piece(6)
    grams.append((re + re_t, im - im_t))
    across = [
        tuple(jnp.sum(jnp.where(lane == row, c, 0.0), axis=0, keepdims=True) for c in coef)
        for coef in coefs
    ]

    def quadratic(first_power):
        out = None
        for l in range(3):
            term = None
            for k in range(3):
                t = cmul_conj(coefs[k], grams[k + l + first_power])
                term = t if term is None else cadd(term, t)
            term = cmul(term, across[l])
            out = term if out is None else cadd(out, term)
        return out

    corr = quadratic(0)
    energy = quadratic(1)
    for i in range(2):
        corr_ref[i] = (corr[i] / cells)[:, :nb]
        en_ref[i] = ((energy[i] + BASE * corr[i]) / cells)[:, :nb]


def on_device(slabs, poles, vectors, potential):
    _, nb, planes, nx, ny = vectors.shape
    rows = nx // poles
    vecs = 2 * nb
    cells = float(planes * slabs * nx * ny)
    vmem = pl.BlockSpec(memory_space=pltpu.VMEM)
    whole = pl.BlockSpec(memory_space=pl.ANY)
    dma = pltpu.SemaphoreType.DMA
    scratch = lambda *shape: pltpu.VMEM(shape, jnp.float32)
    limit = 63 * 1024 * 1024
    basis, packed = pl.pallas_call(
        functools.partial(gather_kernel, slabs, poles),
        out_shape=(
            jax.ShapeDtypeStruct((3, planes, rows, vecs, ny), jnp.float32),
            jax.ShapeDtypeStruct((nb, ny), jnp.float32),
        ),
        in_specs=[whole, whole],
        out_specs=(whole, vmem),
        scratch_shapes=[
            scratch(planes, vecs, nx, ny),
            scratch(planes, nx, ny),
            scratch(planes + 5, rows + 4, vecs, ny),
            scratch(planes + 4, rows + 4, vecs, ny),
            scratch(planes + 1, rows + 1, vecs, ny),
            scratch(3, nx, ny),
            scratch(planes + 4, rows + 4, vecs, ny),
            pltpu.VMEM((8 * vecs, planes * rows * ny), jnp.bfloat16),
            pltpu.VMEM((2 * vecs, planes * rows * ny), jnp.bfloat16),
            scratch(2, nb, ny),
            scratch(slabs, nb, ny),
            scratch(poles, nb, ny),
            dma((planes + 1,)),
            dma((3,)),
            dma((18,)),
            dma((18,)),
            dma((slabs,)),
            dma((slabs,)),
            dma((poles,)),
            dma((poles,)),
        ],
        compiler_params=pltpu.CompilerParams(
            collective_id=0, has_side_effects=True, vmem_limit_bytes=limit
        ),
    )(vectors.reshape(vecs, planes, nx, ny), potential)
    filtered, corr, energy = pl.pallas_call(
        functools.partial(filter_kernel, cells, poles),
        out_shape=(
            jax.ShapeDtypeStruct((vecs * planes * rows, ny), jnp.float32),
            jax.ShapeDtypeStruct((2, nb, nb), jnp.float32),
            jax.ShapeDtypeStruct((2, nb, nb), jnp.float32),
        ),
        in_specs=[whole, vmem],
        out_specs=(vmem, vmem, vmem),
        scratch_shapes=[scratch(3, planes, rows, vecs, ny), dma],
        compiler_params=pltpu.CompilerParams(vmem_limit_bytes=limit),
    )(basis, packed)
    return filtered.reshape(2, nb, planes, rows, ny), corr, energy


def solution(mesh):
    in_specs = (P(None, None, "slab", None, None), P("slab", None, None))
    out_specs = (P(None, None, "slab", "pole", None), P(), P())
    body = functools.partial(on_device, mesh.shape["slab"], mesh.shape["pole"])
    return jax.shard_map(
        body, mesh=mesh, in_specs=in_specs, out_specs=out_specs, check_vma=False
    )
```

```python
import functools
import math

import jax
import jax.numpy as jnp
from jax import lax
from jax.experimental import pallas as pl
from jax.experimental.pallas import tpu as pltpu
from jax.sharding import PartitionSpec as P

ITERS = 3
CENTER = 2.0
RADIUS = 1.5
BASE = 4.0

MESH = pl.DeviceIdType.MESH


def cmul(a, b):
    return (a[0] * b[0] - a[1] * b[1], a[0] * b[1] + a[1] * b[0])


def cmul_conj(a, b):
    return (a[0] * b[0] + a[1] * b[1], a[0] * b[1] - a[1] * b[0])


def cadd(a, b):
    return (a[0] + b[0], a[1] + b[1])


def csub(a, b):
    return (a[0] - b[0], a[1] - b[1])


def cdiv(n, d):
    inv = 1.0 / (d[0] * d[0] + d[1] * d[1])
    return ((n[0] * d[0] + n[1] * d[1]) * inv, (n[1] * d[0] - n[0] * d[1]) * inv)


def cocg_coefficients(moments, shift):
    def form(a, b):
        anti = {}
        for i, ai in enumerate(a):
            for j, bj in enumerate(b):
                term = bj if ai is None else cmul(ai, bj)
                anti[i + j] = cadd(anti[i + j], term) if i + j in anti else term
        total = None
        for n, coef in anti.items():
            term = cmul(coef, moments[n])
            total = term if total is None else cadd(total, term)
        return total

    one = (jnp.ones_like(shift[0]), jnp.zeros_like(shift[0]))
    x = []
    r = [one]
    p = [one]
    rho = moments[0]
    for iteration in range(ITERS):
        q = [cmul(shift, c) for c in p] + [None]
        for i, c in enumerate(p):
            q[i + 1] = (-c[0], -c[1]) if q[i + 1] is None else csub(q[i + 1], c)
        alpha = cdiv(rho, form(p, q))
        step = [cmul(alpha, c) for c in p]
        x = [cadd(x[i], c) if i < len(x) else c for i, c in enumerate(step)]
        if iteration + 1 < ITERS:
            down = [cmul(alpha, c) for c in q]
            r = [csub(r[i], c) if i < len(r) else (-c[0], -c[1]) for i, c in enumerate(down)]
            rho_new = form(r, r)
            beta = cdiv(rho_new, rho)
            p = [cadd(c, cmul(beta, p[i])) if i < len(p) else c for i, c in enumerate(r)]
            rho = rho_new
    return x


def gather_kernel(
    slabs, poles, v_hbm, pot_hbm, basis_hbm, packed_ref,
    v_ref, pot_ref, e0, e1, e2, pot_halo, diag, stack, last, payload, from_slab, from_pole,
    fetch, store, halo_send, halo_recv, slab_send, slab_recv, pole_send, pole_recv,
):
    planes, nx, lanes = pot_ref.shape
    vecs = e0.shape[2]
    nb = vecs // 2
    rows = basis_hbm.shape[2]
    slab = lax.axis_index("slab")
    pole = lax.axis_index("pole")
    x0 = pole * rows
    ahead = lax.rem(pole + 1, poles)
    back = lax.rem(pole + poles - 1, poles)
    up = lax.rem(slab + 1, slabs)
    down = lax.rem(slab + slabs - 1, slabs)

    order = [0, planes - 1] + list(range(1, planes - 1))
    fetches = {
        z: pltpu.make_async_copy(v_hbm.at[:, z], v_ref.at[z], fetch.at[z]) for z in order
    }
    fetch_pot = pltpu.make_async_copy(pot_hbm, pot_ref, fetch.at[planes])
    for z in order:
        fetches[z].start()
    fetch_pot.start()

    barrier = pltpu.get_barrier_semaphore()
    for d in range(1, slabs):
        pl.semaphore_signal(
            barrier, inc=1, device_id={"slab": lax.rem(slab + d, slabs)}, device_id_type=MESH
        )
    for d in range(1, poles):
        pl.semaphore_signal(
            barrier, inc=1, device_id={"pole": lax.rem(pole + d, poles)}, device_id_type=MESH
        )
    empty = jnp.zeros((vecs, stack.shape[1]), stack.dtype)
    stack[pl.ds(3 * vecs, vecs)] = empty
    stack[pl.ds(7 * vecs, vecs)] = empty

    def window(q):
        return lax.rem(x0 + (q - 2 + nx), nx)

    lines = v_ref.reshape(planes * vecs * nx, lanes)

    def gather(z):
        fetches[z].wait()
        for q in range(rows + 4):
            e0[z + 2, q] = lines[pl.ds(z * vecs * nx + window(q), vecs, stride=nx), :]

    copies = []

    def send(i, src, dst, axis, target):
        copy = pltpu.make_async_remote_copy(
            src_ref=src, dst_ref=dst, send_sem=halo_send.at[i], recv_sem=halo_recv.at[i],
            device_id={axis: target}, device_id_type=MESH,
        )
        copy.start()
        copies.append(copy)
        return copy

    own = pl.ds(2, rows)

    def send_plane(i, z, there, target):
        return send(i, e0.at[z + 2, own], e0.at[there + 2, own], "slab", target)

    gather(0)
    gather(planes - 1)
    fetch_pot.wait()
    pl.semaphore_wait(barrier, slabs - 1 + poles - 1)
    near = [
        send_plane(2, planes - 1, -1, up),
        send_plane(3, 0, planes, down),
        send(0, pot_ref.at[planes - 1], pot_halo.at[0], "slab", up),
        send(1, pot_ref.at[0], pot_halo.at[1], "slab", down),
    ]
    for z in range(1, planes - 1):
        gather(z)
    far = [
        send_plane(4, planes - 2, -2, up),
        send_plane(5, 1, planes + 1, down),
    ]

    def spread(ref, z, p):
        for q in range(1, rows + 3):
            line = ref[z, pl.ds(window(q), 1), :] + (3.0 - BASE)
            diag[p, q] = jnp.broadcast_to(line, (vecs, lanes))

    def roll_y(block, by):
        flat = block.reshape(block.shape[0] * vecs, lanes)
        return pltpu.roll(flat, by, 1).reshape(block.shape)

    def apply(src, z, lo, hi):
        p = z + 2
        here = src[p, lo:hi]
        beside = src[p - 1, lo:hi] + src[p + 1, lo:hi]
        beside = beside + src[p, lo - 1:hi - 1] + src[p, lo + 1:hi + 1]
        beside = beside + (roll_y(here, 1) + roll_y(here, lanes - 1))
        return diag[p, lo:hi] * here - 0.5 * beside

    def first_power(z, lo=2, hi=rows + 2):
        e1[z + 2, lo:hi] = apply(e0, z, lo, hi)

    def second_power(z):
        e2[z, :rows] = apply(e1, z, 2, rows + 2)

    def pass_row(i, z, count):
        at = pl.ds(z, count)
        return send(i, e2.at[at, 0], e2.at[at, rows], "pole", back)

    lo, hi = 2, rows + 2
    sums = [None] * 12
    inner, outer = range(1, planes - 1), (0, planes - 1)

    def split(into, high_row, low_row, z, u):
        high = u.astype(jnp.bfloat16)
        low = (u - high.astype(jnp.float32)).astype(jnp.bfloat16)
        for r in range(rows):
            at = pl.ds((z * rows + r) * lanes, lanes)
            into[pl.ds(high_row, vecs), at] = high[r]
            into[pl.ds(low_row, vecs), at] = low[r]

    def collect(n, a, b):
        re = a[:, :nb] * b[:, :nb] - a[:, nb:] * b[:, nb:]
        im = a[:, :nb] * b[:, nb:] + a[:, nb:] * b[:, :nb]
        for i, value in ((n, jnp.sum(re, axis=0)), (6 + n, jnp.sum(im, axis=0))):
            sums[i] = value if sums[i] is None else sums[i] + value

    def own_power(k, z):
        return e2[z, :rows] if k == 2 else (e0, e1)[k][z + 2, lo:hi]

    def take(k, z):
        u = own_power(k, z)
        split(stack, k * vecs, (4 + k) * vecs, z, u)
        if k:
            collect(2 * k - 1, own_power(k - 1, z), u)
        collect(2 * k, u, u)

    def take_last(z):
        u2 = own_power(2, z)
        beside = e2[z + 1, :rows] + e2[z, 1:rows + 1] + roll_y(u2, lanes - 1)
        y = 0.5 * (diag[z + 2, lo:hi] * u2 - beside)
        split(last, 0, vecs, z, y)
        collect(5, u2, y)

    def products(a, b):
        return lax.dot_general(
            a, b, (((1,), (1,)), ((), ())), preferred_element_type=jnp.float32
        )

    def cells_of(z, count):
        return pl.ds(z * rows * lanes, count * rows * lanes)

    def squares(z, count):
        block = stack[:, cells_of(z, count)]
        return products(block, block)

    def last_products(z, count):
        at = cells_of(z, count)
        second = jnp.concatenate(
            [stack[pl.ds(2 * vecs, vecs), at], stack[pl.ds(6 * vecs, vecs), at]], axis=0
        )
        return products(second, last[:, at])

    def fold(full):
        h = full.shape[0] // 2
        return full[:h, :h] + (full[:h, h:] + full[h:, :h] + full[h:, h:])

    for z in range(planes):
        spread(pot_ref, z, z + 2)
    for z in inner:
        first_power(z, 1, rows + 3)
    for z in range(planes):
        take(0, z)
    for z in inner:
        take(1, z)
    for copy in near:
        copy.wait_recv()
    sides = []
    for i, p in ((6, 1), (8, planes + 2)):
        sides.append(send(i, e0.at[p, 2], e0.at[p, rows + 2], "pole", back))
        sides.append(send(i + 1, e0.at[p, rows + 1], e0.at[p, 1], "pole", ahead))
    for z in outer:
        first_power(z)
    spread(pot_halo, 0, 1)
    spread(pot_halo, 1, planes + 2)
    for z in inner:
        second_power(z)
    beside_inner = pass_row(10, 1, planes - 2)
    for z in outer:
        take(1, z)
    for z in inner:
        take(2, z)
    for copy in sides:
        copy.wait_recv()
    for z in outer:
        first_power(z, 1, 2)
        first_power(z, rows + 2, rows + 3)
    for copy in far:
        copy.wait_recv()
    first_power(-1)
    second_power(0)
    edge = send(11, e2.at[0, pl.ds(0, rows)], e2.at[planes, pl.ds(0, rows)], "slab", down)
    first_power(planes)
    second_power(planes - 1)
    beside_outer = [pass_row(12, 0, 1), pass_row(13, planes - 1, 1)]
    stores = [
        pltpu.make_async_copy(src, basis_hbm.at[k], store.at[k])
        for k, src in enumerate((
            e0.at[pl.ds(2, planes), own],
            e1.at[pl.ds(2, planes), own],
            e2.at[pl.ds(0, planes), pl.ds(0, rows)],
        ))
    ]
    for copy in stores:
        copy.start()
    for z in outer:
        take(2, z)
    full = squares(0, planes)
    beside_inner.wait_recv()
    for z in inner:
        take_last(z)
    for copy in beside_outer:
        copy.wait_recv()
    take_last(0)
    m = last_products(0, planes - 1)
    edge.wait_recv()
    take_last(planes - 1)
    m = fold(m + last_products(planes - 1, 1))
    s = fold(full)

    lane = lax.broadcasted_iota(jnp.int32, (nb, lanes), 1)
    row = lax.broadcasted_iota(jnp.int32, (nb, lanes), 0)
    to_left = lanes - nb

    def parts(block):
        re, im = block[:nb], block[nb:]
        return re + pltpu.roll(im, to_left, 1), pltpu.roll(re, to_left, 1) - im

    packed = []
    for k in range(3):
        re, im = parts(s[k * vecs:(k + 1) * vecs])
        packed.append(jnp.where(row <= lax.rem(lane, vecs), re, im))
    pieces = [
        packed[0], pltpu.roll(packed[0], to_left, 1),
        packed[1], pltpu.roll(packed[1], to_left, 1), packed[2],
    ]
    m = jnp.concatenate([m, jnp.zeros((vecs, lanes - vecs), jnp.float32)], axis=1)
    re, im = parts(m)
    pieces += [pltpu.roll(re, 5 * nb, 1), pltpu.roll(im, 6 * nb, 1)]
    out = pieces[0]
    for n in range(1, 7):
        out = jnp.where(lane >= n * nb, pieces[n], out)
    for n in range(12):
        value = jnp.sum(sums[n], axis=1, keepdims=True)
        out = jnp.where(lane == 7 * nb + n, value * (2.0 if n in (5, 11) else 1.0), out)
    payload[0] = out

    def exchange(source, landing, axis, count, me, send_sem, recv_sem):
        sent = []
        for d in range(1, count):
            copy = pltpu.make_async_remote_copy(
                src_ref=source, dst_ref=landing.at[me], send_sem=send_sem.at[d],
                recv_sem=recv_sem.at[d], device_id={axis: lax.rem(me + d, count)},
                device_id_type=MESH,
            )
            copy.start()
            sent.append(copy)
        landing[me] = source[...]
        for copy in sent:
            copy.wait_recv()
        total = landing[0]
        for i in range(1, count):
            total = total + landing[i]
        return total, sent

    total, sent = exchange(payload.at[0], from_pole, "pole", poles, pole, pole_send, pole_recv)
    copies += sent
    payload[1] = total
    total, sent = exchange(payload.at[1], from_slab, "slab", slabs, slab, slab_send, slab_recv)
    copies += sent
    packed_ref[...] = total
    for copy in copies:
        copy.wait_send()
    for copy in stores:
        copy.wait()


def filter_kernel(cells, poles, basis_hbm, packed_ref, f_ref, corr_ref, en_ref, basis, fetch):
    _, planes, rows, vecs, lanes = basis.shape
    nb = vecs // 2
    bring = pltpu.make_async_copy(basis_hbm, basis, fetch)
    bring.start()
    packed = packed_ref[...]
    lane = lax.broadcasted_iota(jnp.int32, (nb, lanes), 1)
    row = lax.broadcasted_iota(jnp.int32, (nb, lanes), 0)

    def column(n):
        at = 7 * nb + n
        return jnp.broadcast_to(packed[:, at:at + 1], (nb, lanes))

    moments = [(column(n), column(6 + n)) for n in range(6)]
    shift_re = jnp.zeros((nb, lanes), jnp.float32)
    shift_im, weight_re, weight_im = shift_re, shift_re, shift_re
    for j in range(poles):
        theta = 2.0 * math.pi / poles * (j + 0.5)
        c, t = math.cos(theta), math.sin(theta)
        here = lane >= 0 if j == 0 else lane == j
        shift_re = jnp.where(here, CENTER - BASE + RADIUS * c, shift_re)
        shift_im = jnp.where(here, RADIUS * t, shift_im)
        weight_re = jnp.where(lane == j, RADIUS * c / poles, weight_re)
        weight_im = jnp.where(lane == j, RADIUS * t / poles, weight_im)
    coefs = []
    for x in cocg_coefficients(moments, (shift_re, shift_im)):
        x = cmul((weight_re, weight_im), x)
        coefs.append(
            tuple(jnp.broadcast_to(jnp.sum(c, axis=1, keepdims=True), (nb, lanes)) for c in x)
        )

    bring.wait()
    for z in range(planes):
        re = im = None
        for (cr, ci), u in zip(coefs, (basis[0, z], basis[1, z], basis[2, z])):
            ur, ui = u[:, :nb], u[:, nb:]
            tr, ti = cr * ur - ci * ui, cr * ui + ci * ur
            re, im = (tr, ti) if re is None else (re + tr, im + ti)
        for r in range(rows):
            both = jnp.concatenate([re[r], im[r]], axis=0)
            f_ref[pl.ds(z * rows + r, vecs, stride=planes * rows), :] = both

    square = jnp.concatenate([packed, jnp.zeros((lanes - nb, lanes), jnp.float32)], axis=0)
    turned = jnp.transpose(square)

    def piece(n):
        here = packed if n == 0 else pltpu.roll(packed, lanes - n * nb, 1)
        return here, turned[n * nb:(n + 1) * nb]

    grams = []
    for n in range(5):
        here, across = piece(n)
        re = jnp.where(row <= lane, here, across)
        im = jnp.where(row > lane, here, jnp.where(row < lane, -across, 0.0))
        grams.append((re, im))
    (re, re_t), (im, im_t) = piece(5), piece(6)
    grams.append((re + re_t, im - im_t))
    across = [
        tuple(jnp.sum(jnp.where(lane == row, c, 0.0), axis=0, keepdims=True) for c in coef)
        for coef in coefs
    ]

    def quadratic(first_power):
        out = None
        for l in range(3):
            term = None
            for k in range(3):
                t = cmul_conj(coefs[k], grams[k + l + first_power])
                term = t if term is None else cadd(term, t)
            term = cmul(term, across[l])
            out = term if out is None else cadd(out, term)
        return out

    corr = quadratic(0)
    energy = quadratic(1)
    for i in range(2):
        corr_ref[i] = (corr[i] / cells)[:, :nb]
        en_ref[i] = ((energy[i] + BASE * corr[i]) / cells)[:, :nb]


def on_device(slabs, poles, vectors, potential):
    _, nb, planes, nx, ny = vectors.shape
    rows = nx // poles
    vecs = 2 * nb
    cells = float(planes * slabs * nx * ny)
    vmem = pl.BlockSpec(memory_space=pltpu.VMEM)
    whole = pl.BlockSpec(memory_space=pl.ANY)
    dma = pltpu.SemaphoreType.DMA
    scratch = lambda *shape: pltpu.VMEM(shape, jnp.float32)
    limit = 63 * 1024 * 1024
    basis, packed = pl.pallas_call(
        functools.partial(gather_kernel, slabs, poles),
        out_shape=(
            jax.ShapeDtypeStruct((3, planes, rows, vecs, ny), jnp.float32),
            jax.ShapeDtypeStruct((nb, ny), jnp.float32),
        ),
        in_specs=[whole, whole],
        out_specs=(whole, vmem),
        scratch_shapes=[
            scratch(planes, vecs, nx, ny),
            scratch(planes, nx, ny),
            scratch(planes + 4, rows + 4, vecs, ny),
            scratch(planes + 4, rows + 4, vecs, ny),
            scratch(planes + 1, rows + 1, vecs, ny),
            scratch(2, nx, ny),
            scratch(planes + 4, rows + 4, vecs, ny),
            pltpu.VMEM((8 * vecs, planes * rows * ny), jnp.bfloat16),
            pltpu.VMEM((2 * vecs, planes * rows * ny), jnp.bfloat16),
            scratch(2, nb, ny),
            scratch(slabs, nb, ny),
            scratch(poles, nb, ny),
            dma((planes + 1,)),
            dma((3,)),
            dma((14,)),
            dma((14,)),
            dma((slabs,)),
            dma((slabs,)),
            dma((poles,)),
            dma((poles,)),
        ],
        compiler_params=pltpu.CompilerParams(
            collective_id=0, has_side_effects=True, vmem_limit_bytes=limit
        ),
    )(vectors.reshape(vecs, planes, nx, ny), potential)
    filtered, corr, energy = pl.pallas_call(
        functools.partial(filter_kernel, cells, poles),
        out_shape=(
            jax.ShapeDtypeStruct((vecs * planes * rows, ny), jnp.float32),
            jax.ShapeDtypeStruct((2, nb, nb), jnp.float32),
            jax.ShapeDtypeStruct((2, nb, nb), jnp.float32),
        ),
        in_specs=[whole, vmem],
        out_specs=(vmem, vmem, vmem),
        scratch_shapes=[scratch(3, planes, rows, vecs, ny), dma],
        compiler_params=pltpu.CompilerParams(vmem_limit_bytes=limit),
    )(basis, packed)
    return filtered.reshape(2, nb, planes, rows, ny), corr, energy


def solution(mesh):
    in_specs = (P(None, None, "slab", None, None), P("slab", None, None))
    out_specs = (P(None, None, "slab", "pole", None), P(), P())
    body = functools.partial(on_device, mesh.shape["slab"], mesh.shape["pole"])
    return jax.shard_map(
        body, mesh=mesh, in_specs=in_specs, out_specs=out_specs, check_vma=False
    )
```
